32 devices in a mesh: dp: 4 (over z), seq: 2 (over x), fsdp: 4 (over y, core).
Axes of the slice: x: 2, y: 2, z: 4, core: 2. Of those that a mesh axis runs over, the one named last changes fastest.
Arguments:
- series_data: float32 [64, 32768], P(('dp', 'fsdp'), 'seq'), may hold values from -6 to 6
- patch_mask: int32 [64, 512], P(('dp', 'fsdp'), 'seq'), may hold values from 0 to 1
- qkv_weight: float32 [2, 512, 1536], P(None, 'fsdp'), may hold values from -0.25 to 0.25
- out_weight: float32 [2, 512, 512], P(None, 'fsdp'), may hold values from -0.75 to 0.75
- up_weight: float32 [2, 512, 2048], P(None, 'fsdp'), may hold values from -0.25 to 0.25
- down_weight: float32 [2, 2048, 512], P(None, 'fsdp'), may hold values from -0.125 to 0.125
- layer_norms: float32 [2, 4, 512], P(None, None, 'fsdp'), may hold values from -0.6 to 1.3, as said below
- embed_weight: float32 [64, 512], P(None, 'fsdp'), may hold values from -0.75 to 0.75
- head_weight: float32 [64, 512], P(None, 'fsdp'), may hold values from -0.25 to 0.25
- pos_table: float32 [512, 512], P(None, 'fsdp'), may hold values from -1.8 to 1.8
- final_norm: float32 [2, 512], P(None, 'fsdp'), may hold values from -0.6 to 1.3, as said below
- qkv_momentum: float32 [2, 512, 1536], P(None, 'fsdp'), may hold values from -0.0006629126 to 0.0006629126
- out_momentum: float32 [2, 512, 512], P(None, 'fsdp'), may hold values from -0.0006629126 to 0.0006629126
- up_momentum: float32 [2, 512, 2048], P(None, 'fsdp'), may hold values from -0.0006629126 to 0.0006629126
- down_momentum: float32 [2, 2048, 512], P(None, 'fsdp'), may hold values from -0.0006629126 to 0.0006629126
- layer_norms_momentum: float32 [2, 4, 512], P(None, None, 'fsdp'), may hold values from -0.006629126 to 0.006629126
- embed_momentum: float32 [64, 512], P(None, 'fsdp'), may hold values from -0.003314563 to 0.003314563
- head_momentum: float32 [64, 512], P(None, 'fsdp'), may hold values from -0.016572814 to 0.016572814
- pos_momentum: float32 [512, 512], P(None, 'fsdp'), may hold values from -0.006629126 to 0.006629126
- final_norm_momentum: float32 [2, 512], P(None, 'fsdp'), may hold values from -0.006629126 to 0.006629126
- qkv_average: float32 [2, 512, 1536], P(None, 'fsdp'), may hold values from -0.25 to 0.25
- out_average: float32 [2, 512, 512], P(None, 'fsdp'), may hold values from -0.75 to 0.75
- up_average: float32 [2, 512, 2048], P(None, 'fsdp'), may hold values from -0.25 to 0.25
- down_average: float32 [2, 2048, 512], P(None, 'fsdp'), may hold values from -0.125 to 0.125
- layer_norms_average: float32 [2, 4, 512], P(None, None, 'fsdp'), may hold values from -0.6 to 1.3
- embed_average: float32 [64, 512], P(None, 'fsdp'), may hold values from -0.75 to 0.75
- head_average: float32 [64, 512], P(None, 'fsdp'), may hold values from -0.25 to 0.25
- pos_average: float32 [512, 512], P(None, 'fsdp'), may hold values from -1.8 to 1.8
- final_norm_average: float32 [2, 512], P(None, 'fsdp'), may hold values from -0.6 to 1.3
Outputs:
- loss_sum: float32 [], replicated
- loss_count: float32 [], replicated
- qkv_new: float32 [2, 512, 1536], P(None, 'fsdp')
- out_new: float32 [2, 512, 512], P(None, 'fsdp')
- up_new: float32 [2, 512, 2048], P(None, 'fsdp')
- down_new: float32 [2, 2048, 512], P(None, 'fsdp')
- layer_norms_new: float32 [2, 4, 512], P(None, None, 'fsdp')
- embed_new: float32 [64, 512], P(None, 'fsdp')
- head_new: float32 [64, 512], P(None, 'fsdp')
- pos_new: float32 [512, 512], P(None, 'fsdp')
- final_norm_new: float32 [2, 512], P(None, 'fsdp')
- qkv_momentum_new: float32 [2, 512, 1536], P(None, 'fsdp')
- out_momentum_new: float32 [2, 512, 512], P(None, 'fsdp')
- up_momentum_new: float32 [2, 512, 2048], P(None, 'fsdp')
- down_momentum_new: float32 [2, 2048, 512], P(None, 'fsdp')
- layer_norms_momentum_new: float32 [2, 4, 512], P(None, None, 'fsdp')
- embed_momentum_new: float32 [64, 512], P(None, 'fsdp')
- head_momentum_new: float32 [64, 512], P(None, 'fsdp')
- pos_momentum_new: float32 [512, 512], P(None, 'fsdp')
- final_norm_momentum_new: float32 [2, 512], P(None, 'fsdp')
- qkv_average_new: float32 [2, 512, 1536], P(None, 'fsdp')
- out_average_new: float32 [2, 512, 512], P(None, 'fsdp')
- up_average_new: float32 [2, 512, 2048], P(None, 'fsdp')
- down_average_new: float32 [2, 2048, 512], P(None, 'fsdp')
- layer_norms_average_new: float32 [2, 4, 512], P(None, None, 'fsdp')
- embed_average_new: float32 [64, 512], P(None, 'fsdp')
- head_average_new: float32 [64, 512], P(None, 'fsdp')
- pos_average_new: float32 [512, 512], P(None, 'fsdp')
- final_norm_average_new: float32 [2, 512], P(None, 'fsdp')
The draws below stay inside these ranges and needn't reach their ends.
Inputs may be any that keep to these rules, and one draw needn't show every extreme that they name: `layer_norms`: rows 0 and 2 are gains, rows 1 and 3 biases. `final_norm`: row 0 is the gain, row 1 the bias.
All inputs are finite; a program needn't handle non-finite values.
Results may differ from the reference program's by a relative error of at most 0.017.
Values may be sent and summed in bfloat16 or wider, within the bound.
A program may use at most 256 MiB of HBM per device.

```python
import math
import jax
import jax.numpy as jnp
from jax import lax

D = 512
FF = 2048
HEADS = 8
HEAD_DIM = 64
PATCH = 64
PATCHES = 512
LAYERS = 2
SER_DEV = 4
SERIES = 64
N_DP = 4
N_SEQ = 2
N_FSDP = 4


def norm_rows(key, pairs):
    gains = 1.0 + 0.3 * jax.random.uniform(jax.random.fold_in(key, 1), (pairs, D), jnp.float32, -1.0, 1.0)
    biases = 0.2 * jax.random.truncated_normal(jax.random.fold_in(key, 2), -3.0, 3.0, (pairs, D), jnp.float32)
    return jnp.stack([gains, biases], axis=1).reshape(pairs * 2, D)


def draw_patch_mask(key, part):
    key = jax.random.fold_in(key, 5)
    series_idx = jnp.arange(SERIES, dtype=jnp.int32)[:, None]
    patch_idx = jnp.arange(PATCHES, dtype=jnp.int32)[None, :]
    owner = series_idx // SER_DEV
    dp_rank = owner // N_FSDP
    fsdp_rank = owner % N_FSDP
    seq_rank = patch_idx // (PATCHES // N_SEQ)
    dp_den = max(N_DP - 1, 1)
    fsdp_den = max(N_FSDP - 1, 1)
    seq_den = max(N_SEQ - 1, 1)
    numer = (dp_den + 2 * dp_rank) * (fsdp_den + 2 * fsdp_rank) * (seq_den + 2 * seq_rank)
    threshold = 330 * numer // (dp_den * fsdp_den * seq_den)
    rolled = jax.random.randint(key, (SERIES, PATCHES), 0, 10000, dtype=jnp.int32)
    return (rolled < threshold).astype(jnp.int32)


def draw_layer_norms(key, part):
    key = jax.random.fold_in(key, 11)
    return norm_rows(key, LAYERS * 2).reshape(LAYERS, 4, D)


def draw_layer_norms_average(key, part):
    key = jax.random.fold_in(key, 12)
    return norm_rows(key, LAYERS * 2).reshape(LAYERS, 4, D)


def draw_final_norm(key, part):
    key = jax.random.fold_in(key, 13)
    return norm_rows(key, 1)


def draw_final_norm_average(key, part):
    key = jax.random.fold_in(key, 14)
    return norm_rows(key, 1)


def shard_levels(key, extent, cuts, low, largest):
    def one(axis_at, shards_of):
        draws = jax.random.uniform(jax.random.fold_in(jax.random.fold_in(key, 6), axis_at), (shards_of,), jnp.float32, low / len(cuts), largest / len(cuts))
        return jnp.repeat(jnp.exp(draws), extent[axis_at] // shards_of).reshape((-1,) + (1,) * (len(extent) - axis_at - 1))

    gain = one(*cuts[0])
    for cut in cuts[1:]:
        gain = gain * one(*cut)
    return gain


def normal_values(key, extent, scale, most, cuts=(), held_as=jnp.bfloat16):
    gain = shard_levels(key, extent, cuts, -0.22, 0.18) if cuts else 1.0
    entries = jax.random.normal(key, extent, jnp.float32) * scale * gain
    return jnp.minimum(jnp.maximum(entries, -most), most).astype(held_as)


def setup_inputs(seed: int = 0) -> dict:
    splits = jax.random.split(jax.random.key(seed), 30)
    return {
        "series_data": normal_values(splits[0], (SERIES, PATCHES * PATCH), 1.0, 6.0, ((0, 16), (1, 2)), jnp.float32),
        "patch_mask": draw_patch_mask(jax.random.fold_in(splits[29], 71), 0),
        "qkv_weight": normal_values(splits[2], (LAYERS, D, 3 * D), D ** -0.5, 0.25, ((1, 4),), jnp.float32),
        "out_weight": normal_values(splits[3], (LAYERS, D, D), (D // 8) ** -0.5, 0.75, ((1, 4),), jnp.float32),
        "up_weight": normal_values(splits[4], (LAYERS, D, FF), D ** -0.5, 0.25, ((1, 4),), jnp.float32),
        "down_weight": normal_values(splits[5], (LAYERS, FF, D), FF ** -0.5, 0.125, ((1, 4),), jnp.float32),
        "layer_norms": draw_layer_norms(jax.random.fold_in(splits[29], 71), 0),
        "embed_weight": normal_values(splits[7], (PATCH, D), PATCH ** -0.5, 0.75, ((1, 4),), jnp.float32),
        "head_weight": normal_values(splits[8], (PATCH, D), D ** -0.5, 0.25, ((1, 4),), jnp.float32),
        "pos_table": normal_values(splits[9], (PATCHES, D), 0.3, 1.8, ((1, 4),), jnp.float32),
        "final_norm": draw_final_norm(jax.random.fold_in(splits[29], 71), 0),
        "qkv_momentum": normal_values(splits[11], (LAYERS, D, 3 * D), (0.02 / (SERIES * PATCHES) ** 0.5), 0.0006629126, ((1, 4),), jnp.float32),
        "out_momentum": normal_values(splits[12], (LAYERS, D, D), (0.02 / (SERIES * PATCHES) ** 0.5), 0.0006629126, ((1, 4),), jnp.float32),
        "up_momentum": normal_values(splits[13], (LAYERS, D, FF), (0.02 / (SERIES * PATCHES) ** 0.5), 0.0006629126, ((1, 4),), jnp.float32),
        "down_momentum": normal_values(splits[14], (LAYERS, FF, D), (0.02 / (SERIES * PATCHES) ** 0.5), 0.0006629126, ((1, 4),), jnp.float32),
        "layer_norms_momentum": normal_values(splits[15], (LAYERS, 4, D), (0.2 / (SERIES * PATCHES) ** 0.5), 0.006629126, ((2, 4),), jnp.float32),
        "embed_momentum": normal_values(splits[16], (PATCH, D), (0.1 / (SERIES * PATCHES) ** 0.5), 0.003314563, ((1, 4),), jnp.float32),
        "head_momentum": normal_values(splits[17], (PATCH, D), (4.0 / (PATCH * D ** 0.5)), 0.016572814, ((1, 4),), jnp.float32),
        "pos_momentum": normal_values(splits[18], (PATCHES, D), (0.2 / (SERIES * PATCHES) ** 0.5), 0.006629126, ((1, 4),), jnp.float32),
        "final_norm_momentum": normal_values(splits[19], (2, D), (0.2 / (SERIES * PATCHES) ** 0.5), 0.006629126, ((1, 4),), jnp.float32),
        "qkv_average": normal_values(splits[20], (LAYERS, D, 3 * D), D ** -0.5, 0.25, ((1, 4),), jnp.float32),
        "out_average": normal_values(splits[21], (LAYERS, D, D), (D // 8) ** -0.5, 0.75, ((1, 4),), jnp.float32),
        "up_average": normal_values(splits[22], (LAYERS, D, FF), D ** -0.5, 0.25, ((1, 4),), jnp.float32),
        "down_average": normal_values(splits[23], (LAYERS, FF, D), FF ** -0.5, 0.125, ((1, 4),), jnp.float32),
        "layer_norms_average": draw_layer_norms_average(jax.random.fold_in(splits[29], 71), 0),
        "embed_average": normal_values(splits[25], (PATCH, D), PATCH ** -0.5, 0.75, ((1, 4),), jnp.float32),
        "head_average": normal_values(splits[26], (PATCH, D), D ** -0.5, 0.25, ((1, 4),), jnp.float32),
        "pos_average": normal_values(splits[27], (PATCHES, D), 0.3, 1.8, ((1, 4),), jnp.float32),
        "final_norm_average": draw_final_norm_average(jax.random.fold_in(splits[29], 71), 0),
    }


NORM_EPS = 1e-05
SCORE_SCALE = 0.125
MOMENTUM_KEEP = 0.9
AVERAGE_KEEP = 0.9
RATE_FACTOR = 0.5

@jax.custom_vjp
def low(v):
    return lax.optimization_barrier(v.astype(jnp.bfloat16)).astype(jnp.float32)

@jax.custom_vjp
def low_back(v):
    return v

def low_keep(v):
    return (low(v), None)

def low_pass(kept, grad):
    return (grad,)

def back_keep(v):
    return (v, None)

def back_low(kept, grad):
    return (low(grad),)
low.defvjp(low_keep, low_pass)
low_back.defvjp(back_keep, back_low)

def matmul_high(left, right):
    return jnp.matmul(left, right, precision=lax.Precision.HIGHEST)

def norm_apply(rows_in, gain_row, bias_row):
    row_mean = lax.optimization_barrier(jnp.mean(rows_in, axis=-1, keepdims=True))
    centred = rows_in - row_mean
    variance = lax.optimization_barrier(jnp.mean(centred * centred, axis=-1, keepdims=True))
    return centred * lax.rsqrt(variance + NORM_EPS) * gain_row + bias_row

def block_loss(params, series_block, mask_block):
    qkv_weight, out_weight, up_weight, down_weight, layer_norms, embed_weight, head_weight, pos_table, final_norm = params
    series_num = series_block.shape[0]
    patches = series_block.reshape(series_num, PATCHES, PATCH)
    masked = mask_block.astype(jnp.float32)[..., None]
    inputs = low(patches * (1.0 - masked))
    hidden = low_back(matmul_high(inputs, low(embed_weight))) + pos_table
    for layer_no in range(LAYERS):
        norm_row = layer_norms[layer_no]
        normed = low(norm_apply(hidden, norm_row[0], norm_row[1]))
        qkv_all = low(low_back(matmul_high(normed, low(qkv_weight[layer_no]))))
        queries = qkv_all[..., :D].reshape(series_num, PATCHES, HEADS, HEAD_DIM)
        key_all = qkv_all[..., D:2 * D].reshape(series_num, PATCHES, HEADS, HEAD_DIM)
        value_all = qkv_all[..., 2 * D:].reshape(series_num, PATCHES, HEADS, HEAD_DIM)
        scores = low_back(jnp.einsum('bnhe,bmhe->bhnm', queries, key_all, precision=lax.Precision.HIGHEST) * SCORE_SCALE)
        softmax_w = low(jax.nn.softmax(scores, axis=-1))
        context = jnp.einsum('bhnm,bmhe->bnhe', softmax_w, value_all, precision=lax.Precision.HIGHEST)
        context = low(low_back(context.reshape(series_num, PATCHES, D)))
        hidden = hidden + low_back(matmul_high(context, low(out_weight[layer_no])))
        normed2 = low(norm_apply(hidden, norm_row[2], norm_row[3]))
        up_proj = low_back(matmul_high(normed2, low(up_weight[layer_no])))
        active = low(low_back(jax.nn.gelu(up_proj)))
        hidden = hidden + low_back(matmul_high(active, low(down_weight[layer_no])))
    final_rows = low(norm_apply(hidden, final_norm[0], final_norm[1]))
    predicted = low_back(matmul_high(final_rows, low(head_weight).T))
    errors = predicted - patches
    return jnp.sum(errors * errors * masked)

def advance(weight, gradient, momentum, average, step_rate):
    new_momentum = MOMENTUM_KEEP * momentum + gradient
    new_weight = weight - step_rate * (gradient + MOMENTUM_KEEP * new_momentum)
    new_average = AVERAGE_KEEP * average + (1.0 - AVERAGE_KEEP) * new_weight
    return (new_weight, new_momentum, new_average)

def reference(series_data, patch_mask, qkv_weight, out_weight, up_weight, down_weight, layer_norms, embed_weight, head_weight, pos_table, final_norm, qkv_momentum, out_momentum, up_momentum, down_momentum, layer_norms_momentum, embed_momentum, head_momentum, pos_momentum, final_norm_momentum, qkv_average, out_average, up_average, down_average, layer_norms_average, embed_average, head_average, pos_average, final_norm_average):
    params = (qkv_weight, out_weight, up_weight, down_weight, layer_norms, embed_weight, head_weight, pos_table, final_norm)
    moments = (qkv_momentum, out_momentum, up_momentum, down_momentum, layer_norms_momentum, embed_momentum, head_momentum, pos_momentum, final_norm_momentum)
    averages = (qkv_average, out_average, up_average, down_average, layer_norms_average, embed_average, head_average, pos_average, final_norm_average)
    loss_count = jnp.sum(patch_mask.astype(jnp.float32)) * PATCH
    back_scale = jnp.float32(1.0) / loss_count
    block_count = SERIES // 8
    data_blocks = series_data.reshape(block_count, 8, PATCHES * PATCH)
    mask_blocks = patch_mask.reshape(block_count, 8, PATCHES)
    checked = jax.checkpoint(block_loss)

    def one_block(carry, pieces):
        total, grads = carry
        loss_part, pull_back = jax.vjp(lambda weights_in: checked(weights_in, pieces[0], pieces[1]), params)
        got = pull_back(back_scale.astype(loss_part.dtype))[0]
        grads = jax.tree.map(lambda left, right: left + right, grads, got)
        return ((total + loss_part, grads), None)
    zero_grads = jax.tree.map(jnp.zeros_like, params)
    (loss_sum, grads), _ = lax.scan(one_block, (jnp.zeros((), jnp.float32), zero_grads), (data_blocks, mask_blocks))
    step_rate = RATE_FACTOR * math.sqrt(SERIES * PATCHES)
    results = [advance(params[member], grads[member], moments[member], averages[member], step_rate) for member in range(9)]
    new_w = [entry[0] for entry in results]
    new_m = [entry[1] for entry in results]
    new_a = [entry[2] for entry in results]
    return (loss_sum, loss_count, new_w[0], new_w[1], new_w[2], new_w[3], new_w[4], new_w[5], new_w[6], new_w[7], new_w[8], new_m[0], new_m[1], new_m[2], new_m[3], new_m[4], new_m[5], new_m[6], new_m[7], new_m[8], new_a[0], new_a[1], new_a[2], new_a[3], new_a[4], new_a[5], new_a[6], new_a[7], new_a[8])
```

```python
import functools
import math

import jax
import jax.numpy as jnp
from jax import lax
from jax.experimental import pallas as pl
from jax.experimental.pallas import tpu as pltpu
from jax.sharding import PartitionSpec as P

D = 512
HEADS = 8
HEAD_DIM = 64
PATCH = 64
PATCHES = 512
LAYERS = 2
NORM_EPS = 1e-05
SCORE_SCALE = 0.125
MOMENTUM_KEEP = 0.9
AVERAGE_KEEP = 0.9
RATE_FACTOR = 0.5
MESH = pl.DeviceIdType.MESH
VMEM_LIMIT = 60 * 2**20


def flip(index, bit):
    return index + bit - 2 * bit * ((index // bit) % 2)


def position():
    return lax.axis_index("dp"), lax.axis_index("seq"), lax.axis_index("fsdp")


def bits_of(extent):
    found = []
    bit = 1
    while bit < extent:
        found.append(bit)
        bit *= 2
    return found


def greet(partners):
    barrier = pltpu.get_barrier_semaphore()
    for partner in partners:
        pl.semaphore_signal(barrier, inc=1, device_id=partner, device_id_type=MESH)
    pl.semaphore_wait(barrier, len(partners))


def remote(src, dst, send_sem, recv_sem, partner):
    return pltpu.make_async_remote_copy(
        src_ref=src,
        dst_ref=dst,
        send_sem=send_sem,
        recv_sem=recv_sem,
        device_id=partner,
        device_id_type=MESH,
    )

RB = 256
SERIES_ROWS = 512
GELU_A = math.sqrt(2.0 / math.pi)
GELU_B = 0.044715


def dot_nn(left, right):
    return jnp.dot(left, right, preferred_element_type=jnp.float32)


def dot_nt(left, right):
    return lax.dot_general(left, right, (((1,), (1,)), ((), ())), preferred_element_type=jnp.float32)


def dot_tn(left, right):
    return lax.dot_general(left, right, (((0,), (0,)), ((), ())), preferred_element_type=jnp.float32)


def low(value):
    return value.astype(jnp.bfloat16)


def wide(value):
    return value.astype(jnp.float32)


def normalise(rows):
    centred = rows - jnp.mean(rows, axis=-1, keepdims=True)
    variance = jnp.mean(centred * centred, axis=-1, keepdims=True)
    inverse = lax.rsqrt(variance + NORM_EPS)
    return centred * inverse, inverse


def norm_back(grad_rows, scaled, inverse, gain):
    inner = grad_rows * gain
    first = jnp.mean(inner, axis=-1, keepdims=True)
    second = jnp.mean(inner * scaled, axis=-1, keepdims=True)
    return inverse * (inner - first - scaled * second)


def column_sum(value):
    return jnp.sum(value, axis=0, keepdims=True)


def matrix(square, l, j):
    return square[l, j].reshape(512, 512)


def row_block(index, size=RB):
    return pl.ds(pl.multiple_of(index * size, size), size)


def forward_in(l, refs):
    small, square, tall, hid, mid, qkv, lse, ctx, up = refs
    gain, bias = wide(small[640 + 4 * l : 641 + 4 * l]), wide(small[641 + 4 * l : 642 + 4 * l])

    def body(i, carry):
        r = row_block(i)
        normed = low(normalise(hid[l, r])[0] * gain + bias)
        for j in range(3):
            got = dot_nn(normed, matrix(square, l, j))
            if j == 0:
                got = got * SCORE_SCALE
            qkv[l, j, r] = low(got)
        return carry

    lax.fori_loop(0, hid.shape[1] // RB, body, 0)


def pair_slices(index):
    series, pair = index // 4, index % 4
    return row_block(series, SERIES_ROWS), pl.ds(pl.multiple_of(128 * pair, 128), 128)


def head_mask(block, head):
    lane = lax.broadcasted_iota(jnp.int32, block.shape, 1)
    keep = lane < HEAD_DIM if head == 0 else lane >= HEAD_DIM
    return jnp.where(keep, block, jnp.zeros_like(block))


def forward_attention(l, refs, hook):
    small, square, tall, hid, mid, qkv, lse, ctx, up = refs

    def body(index, carry):
        r, columns = pair_slices(index)
        query, key, value = (qkv[l, part, r, columns] for part in range(3))
        value_t = value.T
        parts = []
        for head in range(2):
            scores = dot_nt(head_mask(key, head), query)
            top = jnp.max(scores, axis=0, keepdims=True)
            weights = jnp.exp(scores - top)
            total = column_sum(weights)
            lse[l, index, head : head + 1] = top + jnp.log(total)
            part = dot_nn(value_t[64 * head : 64 * head + 64], low(weights))
            parts.append(part * (1.0 / total))
        ctx[l, r, columns] = low(jnp.concatenate(parts, axis=0).T)
        return carry

    split_loop(body, lse.shape[1], 2, hook)


def forward_out(l, refs, target, hook):
    small, square, tall, hid, mid, qkv, lse, ctx, up = refs
    gain, bias = wide(small[642 + 4 * l : 643 + 4 * l]), wide(small[643 + 4 * l : 644 + 4 * l])

    def body(i, carry):
        r = row_block(i)
        middle = hid[l, r] + dot_nn(ctx[l, r], matrix(square, l, 3))
        mid[l, r] = middle
        normed = low(normalise(middle)[0] * gain + bias)
        result = middle
        for j in range(4):
            raised = dot_nn(normed, matrix(square, l, 4 + j))
            up[l, j, r] = low(raised)
            bend = jnp.tanh(GELU_A * (raised + GELU_B * raised * raised * raised))
            active = low(0.5 * raised * (1.0 + bend))
            result = result + dot_nn(active, tall[l, j // 2, j % 2].reshape(512, 512))
        target[r] = result
        return carry

    split_loop(body, hid.shape[1] // RB, 2, hook)


def masked_input(block):
    lane = lax.broadcasted_iota(jnp.int32, block.shape, 1)
    hidden = block * (1.0 - pltpu.roll(block, 64, 1))
    return low(jnp.where(lane < PATCH, hidden, 0.0))


def split_loop(body, count, parts, hook):
    size = count // parts
    for part in range(parts):
        lax.fori_loop(part * size, (part + 1) * size, body, 0)
        hook()


def embed(rows, small, hid):
    def body(i, carry):
        r = row_block(i)
        place = pl.ds(pl.multiple_of(128 + (i * RB) % PATCHES, 128), RB)
        hid[0, r] = dot_nn(masked_input(rows[r]), small[0:128]) + wide(small[place])
        return carry

    lax.fori_loop(0, hid.shape[1] // RB, body, 0)


def top(rows, small, grad, head_grad, norm_grad, sums):
    gain, bias = wide(small[648:649]), wide(small[649:650])
    head_grad[...] = jnp.zeros_like(head_grad)

    def body(i, carry):
        loss, count, gain_sum, bias_sum = carry
        r = row_block(i)
        block = rows[r]
        lane = lax.broadcasted_iota(jnp.int32, block.shape, 1)
        mask = jnp.where(lane >= PATCH, block, 0.0)
        scaled, inverse = normalise(grad[r])
        final = low(scaled * gain + bias)
        errors = dot_nt(final, small[0:128]) - pltpu.roll(block, 64, 1)
        wrong = errors * mask
        pull = low(2.0 * wrong)
        head_grad[...] += dot_tn(pull, final)
        below = dot_nn(pull, small[0:128])
        grad[r] = norm_back(below, scaled, inverse, gain)
        return (
            loss + column_sum(errors * wrong),
            count + column_sum(mask),
            gain_sum + column_sum(below * scaled),
            bias_sum + column_sum(below),
        )

    zero, line = jnp.zeros((1, 512), jnp.float32), jnp.zeros((1, 128), jnp.float32)
    loss, count, gain_sum, bias_sum = lax.fori_loop(
        0, grad.shape[0] // RB, body, (line, line, zero, zero)
    )
    norm_grad[8:9] = gain_sum
    norm_grad[9:10] = bias_sum
    lane = lax.broadcasted_iota(jnp.int32, (8, 128), 1)
    sums[...] = jnp.where(lane == 0, jnp.sum(loss), jnp.where(lane == 1, jnp.sum(count), 0.0))


def backward_mlp(l, refs, grad, act, back16, mid16, normed16, dctx, norm_grad, hook):
    small, square, tall, hid, mid, qkv, lse, ctx, up = refs
    gain, bias = wide(small[642 + 4 * l : 643 + 4 * l]), wide(small[643 + 4 * l : 644 + 4 * l])

    def body(i, carry):
        r = row_block(i)
        upstream = grad[r]
        upstream16 = low(upstream)
        back16[r] = upstream16
        below = jnp.zeros((RB, 512), jnp.float32)
        for j in range(4):
            pulled = wide(
                low(dot_nt(upstream16, tall[l, j // 2, j % 2].reshape(512, 512)))
            )
            raised = wide(up[l, j, r])
            square_u = raised * raised
            bend = jnp.tanh(GELU_A * (raised + GELU_B * raised * square_u))
            half = 0.5 * (1.0 + bend)
            act[j, r] = low(raised * half)
            slope = half + (0.5 * GELU_A) * raised * (1.0 - bend * bend) * (
                1.0 + (3.0 * GELU_B) * square_u
            )
            inner = low(pulled * slope)
            up[l, j, r] = inner
            below = below + dot_nt(inner, matrix(square, l, 4 + j))
        scaled, inverse = normalise(mid[l, r])
        middle = upstream + norm_back(below, scaled, inverse, gain)
        grad[r] = middle
        middle16 = low(middle)
        mid16[r] = middle16
        normed16[r] = low(scaled * gain + bias)
        dctx[r] = low(dot_nt(middle16, matrix(square, l, 3)))
        norm_grad[4 * l + 2 : 4 * l + 3] += column_sum(below * scaled)
        norm_grad[4 * l + 3 : 4 * l + 4] += column_sum(below)
        return carry

    split_loop(body, grad.shape[0] // RB, 4, hook)


def weights_mlp(l, refs, act, back16, mid16, normed16, hook):
    small, square, tall, hid, mid, qkv, lse, ctx, up = refs
    for j in range(4):
        tile = low(dot_tn(normed16[...], up[l, j]))
        square[l, 4 + j] = tile.reshape(2, 2, 128, 512)
        if j == 1:
            hook()
    for j in range(4):
        tile = low(dot_tn(act[j], back16[...]))
        tall[l, j // 2, j % 2] = tile.reshape(4, 128, 512)
        if j == 1:
            hook()
    square[l, 3] = low(dot_tn(ctx[l], mid16[...])).reshape(2, 2, 128, 512)


def backward_attention(l, refs, dctx, hook):
    small, square, tall, hid, mid, qkv, lse, ctx, up = refs

    def body(index, carry):
        r, columns = pair_slices(index)
        query, key, value = (qkv[l, part, r, columns] for part in range(3))
        pulled = dctx[r, columns]
        key_t = key.T
        queries_t, keys, values = [], [], []
        for head in range(2):
            scores = dot_nt(head_mask(key, head), query)
            weights = jnp.exp(scores - lse[l, index, head : head + 1])
            grad_weights = dot_nt(head_mask(value, head), pulled)
            inner = weights * grad_weights
            grad_scores = low(inner - weights * column_sum(inner))
            values.append(dot_nn(low(weights), pulled))
            keys.append(dot_nn(grad_scores, query))
            queries_t.append(dot_nn(key_t[64 * head : 64 * head + 64], grad_scores))
        lane = lax.broadcasted_iota(jnp.int32, (SERIES_ROWS, 128), 1)
        qkv[l, 0, r, columns] = low(jnp.concatenate(queries_t, axis=0).T * SCORE_SCALE)
        qkv[l, 1, r, columns] = low(jnp.where(lane < HEAD_DIM, keys[0], keys[1]))
        qkv[l, 2, r, columns] = low(jnp.where(lane < HEAD_DIM, values[0], values[1]))
        return carry

    split_loop(body, lse.shape[1], 4, hook)


def backward_in(l, refs, grad, normed16, norm_grad, hook):
    small, square, tall, hid, mid, qkv, lse, ctx, up = refs
    gain, bias = wide(small[640 + 4 * l : 641 + 4 * l]), wide(small[641 + 4 * l : 642 + 4 * l])

    def body(i, carry):
        r = row_block(i)
        below = dot_nt(qkv[l, 0, r], matrix(square, l, 0))
        for j in range(1, 3):
            below = below + dot_nt(qkv[l, j, r], matrix(square, l, j))
        scaled, inverse = normalise(hid[l, r])
        grad[r] = grad[r] + norm_back(below, scaled, inverse, gain)
        normed16[r] = low(scaled * gain + bias)
        norm_grad[4 * l : 4 * l + 1] += column_sum(below * scaled)
        norm_grad[4 * l + 1 : 4 * l + 2] += column_sum(below)
        return carry

    split_loop(body, grad.shape[0] // RB, 2, hook)


def weights_in(l, refs, normed16):
    square, qkv = refs[1], refs[5]
    for j in range(3):
        square[l, j] = low(dot_tn(normed16[...], qkv[l, j])).reshape(2, 2, 128, 512)


def small_grads(rows, grad, head_grad, norm_grad, store):
    def put(first, block):
        for owner in range(4):
            store[owner // 2, owner % 2, first : first + block.shape[0]] = low(
                block[:, 128 * owner : 128 * owner + 128]
            )

    total = head_grad[...]
    for i in range(rows.shape[0] // 512):
        r = slice(512 * i, 512 * i + 512)
        total = total + dot_tn(masked_input(rows[r]), low(grad[r]))
    put(0, total)
    summed = grad[0:512]
    for i in range(1, rows.shape[0] // 512):
        summed = summed + grad[512 * i : 512 * i + 512]
    put(128, summed)
    put(640, norm_grad[...])
    for owner in range(4):
        store[owner // 2, owner % 2, 656:768] = jnp.zeros((112, 128), jnp.bfloat16)


def run_gather(position_now, weights, smalls, square, tall, small, stage, sems):
    dp, seq, high, low_bit = position_now
    fsdp = 2 * high + low_bit
    send_sem, recv_sem, stage_sem = sems
    core = (dp, seq, 2 * high + 1 - low_bit)
    other = (dp, seq, 2 * (1 - high) + low_bit)
    twin = (dp, 1 - seq, fsdp)
    qkv_w, out_w, up_w, down_w = weights

    def lanes(owner):
        return pl.ds(pl.multiple_of(128 * owner, 128), 128)

    def small_full(y, c):
        return small.at[:, lanes(2 * y + c)]

    def small_part(y, c, half):
        return small.at[pl.ds(pl.multiple_of(384 * half, 128), 384), lanes(2 * y + c)]

    places = [(small_full, small_part)]
    for l in range(LAYERS):
        for first, number in ((0, 3), (3, 1), (4, 4)):
            places.append(
                (
                    lambda y, c, l=l, js=pl.ds(first, number): square.at[l, js, y, c],
                    lambda y, c, half, l=l, js=pl.ds(first, number): square.at[
                        l, js, y, c, pl.ds(pl.multiple_of(64 * half, 64), 64)
                    ],
                )
            )
        places.append(
            (
                lambda y, c, l=l: tall.at[l, y, c],
                lambda y, c, half, l=l: tall.at[l, y, c, pl.ds(2 * half, 2)],
            )
        )

    def copies(number):
        full, part = places[number]
        near, far = (high, low_bit), (1 - high, low_bit)
        moves = [
            (full(*near), core),
            (part(*near, seq), other),
            (part(*far, seq), twin),
            (part(*far, seq), core),
            (part(*far, 1 - seq), core),
        ]
        return [
            remote(ref, ref, send_sem.at[number, kind], recv_sem.at[number, kind], partner)
            for kind, (ref, partner) in enumerate(moves)
        ]

    every = [copies(number) for number in range(len(places))]

    staged = []
    for l in range(LAYERS):
        moves = [(qkv_w.at[l, :, pl.ds(512 * j, 512)], j, 1) for j in range(3)]
        moves += [(out_w.at[l], 3, 1)]
        moves += [(up_w.at[l, :, pl.ds(512 * j, 512)], 4 + j, 1) for j in range(4)]
        moves += [(down_w.at[l], 8, 4)]
        for index, (src, first, number) in enumerate(moves):
            dst = stage(l, first, number)
            copy = pltpu.make_async_copy(src, dst, stage_sem.at[l, index])
            copy.start()
            staged.append((copy, l, first, number, dst))

    embed_w, head_w, pos_w, norms_w, final_w = smalls
    mine = lanes(fsdp)
    small[0:64, mine] = low(embed_w[...])
    small[64:128, mine] = low(head_w[...])
    small[128:640, mine] = low(pos_w[...])
    small[640:656, mine] = low(jnp.concatenate([norms_w[...], final_w[...], jnp.zeros((6, 128))]))
    small[656:768, mine] = jnp.zeros((112, 128), jnp.bfloat16)

    def launch(number):
        every[number][1].start()
        every[number][0].start()

    def launch_rest():
        ends = {2: 1, 3: 2, 7: 3, 8: 4}
        for copy, l, first, number, dst in staged:
            copy.wait()
            if first < 8:
                square[l, first, high, low_bit] = low(dst[...])
            else:
                tall[l, high, low_bit] = low(dst[...]).reshape(4, 128, 512)
            if first in ends:
                launch(4 * l + ends[first])

    queue = []
    for number in range(len(places) + 1):
        if number < len(places):
            queue.append((1, number))
        if number > 0:
            queue.append((2, number - 1))

    def pump(steps):
        for _ in range(min(steps, len(queue))):
            kind, number = queue.pop(0)
            every[number][kind].wait_recv()
            if kind == 1:
                every[number][2].start()
                every[number][3].start()
            else:
                every[number][4].start()

    def finish(number):
        while (2, number) in queue:
            pump(1)
        for kind in (0, 3, 4):
            every[number][kind].wait_recv()

    def close():
        for entry in every:
            for copy in entry:
                copy.wait_send()

    return launch, launch_rest, pump, finish, close


def run_reduce(position_now, dp_bits, buffers, ready, sems):
    dp, seq, high, low_bit = position_now
    fsdp = 2 * high + low_bit
    core = (dp, seq, 2 * high + 1 - low_bit)
    other = (dp, seq, 2 * (1 - high) + low_bit)
    twin = (dp, 1 - seq, fsdp)
    lines = [(flip(dp, bit), seq, fsdp) for bit in dp_bits]
    square, tall, up, qkv, ctx, small_store, landing, out_big, out_small = buffers
    ready_core, ready_other = ready
    send_sem, recv_sem = sems
    first_land = up.reshape(2, 8, 2, 2, 128, 512)
    second_land = qkv.reshape(2, 12, 2, 128, 512)
    early_land = ctx.reshape(2, 4, 2, 128, 512)

    def describe(n):
        if n == 12:
            small_land = landing[1::2]
            return dict(
                source=lambda lane: small_store.at[:, lane],
                land=[small_land[0], small_land[1]] + list(small_land[2:]),
                of_y=lambda ref, y: ref.at[y],
                half=lambda ref, s: ref.at[pl.ds(pl.multiple_of(384 * s, 128), 384)],
                final=out_small,
                rows=384,
            )
        l, k = 1 - n // 6, n % 6
        if k in (2, 3):
            source = lambda lane: tall.at[l, :, lane, pl.ds(2 * (k - 2), 2)]
            of_y = lambda ref, y: ref.at[y]
        else:
            first = (4, 6, None, None, 0, 2)[k]
            source = lambda lane: square.at[l, pl.ds(first, 2), :, lane]
            of_y = lambda ref, y: ref.at[:, y]
        second = early_land.at[1, n] if n < 4 else second_land.at[1, n - 4]
        return dict(
            source=source,
            land=[first_land.at[l, k], second] + [ref.at[n] for ref in landing[4::2]],
            of_y=of_y,
            half=lambda ref, s: ref.at[s],
            final=out_big.at[n],
            rows=128,
        )

    chunks = [describe(n) for n in range(13)]
    pending, started = {}, []

    def begin(n, step, src, dst, partner):
        copy = remote(src, dst, send_sem.at[n, step], recv_sem.at[n, step], partner)
        copy.start()
        started.append(copy)
        pending[n] = copy

    def advance_chunk(n, step):
        chunk = chunks[n]
        land = chunk["land"]
        plan = reduce_plan(dp_bits, chunk["rows"])
        if step > 0:
            pending.pop(n).wait_recv()
        if step == 0:
            if n in (0, 6):
                pl.semaphore_wait(ready_core.at[n // 6], 1)
            begin(n, step, chunk["source"](1 - low_bit), land[0], core)
            return
        if step == 1:
            land[0][...] += chunk["source"](low_bit)[...]
            if n in (0, 4):
                pl.semaphore_wait(ready_other.at[n // 4], 1)
            begin(n, step, chunk["of_y"](land[0], 1 - high), land[1], other)
            return
        if step == 2:
            land[1][...] += chunk["of_y"](land[0], high)[...]
            begin(n, step, chunk["half"](land[1], 1 - seq), land[2], twin)
            return
        if step == 3:
            land[2][...] += chunk["half"](land[1], seq)[...]
        at = step - 3
        offset, starts = 0, []
        for bit, kept in plan:
            side = (dp // bit) % 2
            starts.append(offset + side * kept)
            offset = offset + side * kept
        final = chunk["half"](chunk["final"], seq)
        if at <= len(plan):
            if at > 0:
                bit, kept = plan[at - 1]
                previous = land[1 + at]
                if kept:
                    side = (dp // bit) % 2
                    previous = previous.at[pl.ds(pl.multiple_of(side * kept, 16), kept)]
                land[2 + at][...] += previous[...]
            held = land[2 + at]
            if at < len(plan):
                bit, kept = plan[at]
                src = held
                if kept:
                    side = (dp // bit) % 2
                    src = held.at[pl.ds(pl.multiple_of((1 - side) * kept, 16), kept)]
                begin(n, step, src, land[3 + at], lines[at])
                return
            final[pl.ds(pl.multiple_of(offset, 16), held.shape[0])] = held[...]
        back = [index for index in range(len(plan)) if plan[index][1]][::-1]
        turn = at - len(plan)
        if turn < len(back):
            index = back[turn]
            piece = final.at[pl.ds(pl.multiple_of(starts[index], 16), plan[index][1])]
            begin(n, step, piece, piece, lines[index])
        elif turn == len(back):
            begin(n, step, final, final, twin)

    progress = [0] * 13
    last = []
    for chunk in chunks:
        plan = reduce_plan(dp_bits, chunk["rows"])
        last.append(4 + len(plan) + sum(1 for entry in plan if entry[1]))
    allowed = [0]

    def tick():
        fresh = False
        for n in range(allowed[0]):
            if progress[n] > last[n] or (progress[n] == 0 and fresh):
                continue
            fresh = fresh or progress[n] == 0
            advance_chunk(n, progress[n])
            progress[n] += 1

    def allow(count):
        allowed[0] = count

    def drain():
        while any(progress[n] <= last[n] for n in range(13)):
            tick()
        for copy in started:
            copy.wait_send()

    def ready_for(partner, semaphore):
        pl.semaphore_signal(semaphore, inc=1, device_id=partner, device_id_type=MESH)

    return tick, allow, drain, lambda i: ready_for(core, ready_core.at[i]), lambda i: ready_for(
        other, ready_other.at[i]
    )


def reduce_plan(dp_bits, rows):
    plan = []
    for bit in dp_bits:
        if rows % 32 == 0:
            rows //= 2
            plan.append((bit, rows))
        else:
            plan.append((bit, 0))
    return plan


def mega_kernel(dp_bits, landings, *refs):
    rows_in, qkv_w, out_w, up_w, down_w, embed_w, head_w, pos_w, norms_w, final_w = refs[:10]
    out_big, out_small, out_sums = refs[10:13]
    (rows, small, square, tall, hid, mid, qkv, lse, ctx, up, grad, act, back16, mid16, normed16,
     dctx, head_grad, norm_grad, small_store, loss_land) = refs[13:33]
    landing = refs[33 : 33 + landings]
    (gather_send, gather_recv, stage_sem, rows_sem, rows_local, reduce_send, reduce_recv, loss_send,
     loss_recv, ready_core, ready_other) = refs[33 + landings :]
    dp, seq, fsdp = position()
    high, low_bit = fsdp // 2, fsdp % 2
    place = (dp, seq, high, low_bit)
    core = (dp, seq, 2 * high + 1 - low_bit)
    other = (dp, seq, 2 * (1 - high) + low_bit)
    twin = (dp, 1 - seq, fsdp)
    partners = [core, other, twin] + [(flip(dp, bit), seq, fsdp) for bit in dp_bits]

    def stage(l, first, number):
        if first < 8:
            return mid.at[l, pl.ds(128 * first, 128 * number)]
        return (hid.at[1] if l == 0 else grad).at[pl.ds(0, 512)]

    launch, launch_rest, pump, finish, close = run_gather(
        place,
        (qkv_w, out_w, up_w, down_w),
        (embed_w, head_w, pos_w, norms_w, final_w),
        square,
        tall,
        small,
        stage,
        (gather_send, gather_recv, stage_sem),
    )
    greet(partners)
    launch(0)
    keep, local = rows_in.shape[0] // 2, rows_in.shape[1]
    mine = rows.at[:, pl.ds(pl.multiple_of(local * seq, local), local)]
    trade = remote(
        rows_in.at[pl.ds(keep * (1 - seq), keep)], mine, rows_sem.at[0], rows_sem.at[1], twin
    )
    trade.start()
    own = pltpu.make_async_copy(rows_in.at[pl.ds(keep * seq, keep)], mine, rows_local.at[0])
    own.start()
    launch_rest()
    norm_grad[...] = jnp.zeros_like(norm_grad)
    pump(3)
    finish(0)
    own.wait()
    trade.wait()

    parts = (small, square, tall, hid, mid, qkv, lse, ctx, up)
    flat_rows = rows.reshape(rows.shape[0] * rows.shape[1], 128)
    embed(flat_rows, small, hid)
    for l in range(LAYERS):
        finish(4 * l + 1)
        forward_in(l, parts)
        pump(2)
        forward_attention(l, parts, lambda: pump(2))
        for number in range(4 * l + 2, 4 * l + 5):
            finish(number)
        forward_out(l, parts, hid.at[1] if l == 0 else grad, lambda: pump(2))
    close()
    top(flat_rows, small, grad, head_grad, norm_grad, loss_land.at[0])

    tick, allow, drain, ready_to_core, ready_to_other = run_reduce(
        place,
        dp_bits,
        (square, tall, up, qkv, ctx, small_store, landing, out_big, out_small),
        (ready_core, ready_other),
        (reduce_send, reduce_recv),
    )
    loss_state = {}
    loss_step = [0]

    def loss_tick():
        step = loss_step[0]
        if step > len(partners):
            return
        loss_step[0] += 1
        if step > 0:
            loss_state[step - 1].wait_recv()
            loss_land[2 * step] = loss_land[2 * step - 2] + loss_land[2 * step - 1]
        if step < len(partners):
            loss_state[step] = remote(
                loss_land.at[2 * step],
                loss_land.at[2 * step + 1],
                loss_send.at[step],
                loss_recv.at[step],
                partners[step],
            )
            loss_state[step].start()
        else:
            out_sums[...] = loss_land[2 * step]

    def hook():
        tick()
        loss_tick()

    for l in reversed(range(LAYERS)):
        backward_mlp(l, parts, grad, act, back16, mid16, normed16, dctx, norm_grad, hook)
        weights_mlp(l, parts, act, back16, mid16, normed16, hook)
        ready_to_core(1 - l)
        if l == 1:
            ready_to_other(0)
        allow(4 if l == 1 else 10)
        backward_attention(l, parts, dctx, hook)
        backward_in(l, parts, grad, normed16, norm_grad, hook)
        weights_in(l, parts, normed16)
        if l == 1:
            ready_to_other(1)
        allow(6 if l == 1 else 12)
        hook()
    small_grads(flat_rows, grad, head_grad, norm_grad, small_store)
    allow(13)
    while loss_step[0] <= len(partners):
        loss_tick()
    drain()
    for copy in loss_state.values():
        copy.wait_send()


def mega_call(rows, weights, smalls, dp_extent):
    dp_bits = bits_of(dp_extent)
    levels = 3 + len(dp_bits)
    number = rows.shape[0] * rows.shape[1]
    keep = rows.shape[0] // 2
    pairs = keep * 4
    f32, b16 = jnp.float32, jnp.bfloat16
    landing = [(8, 128), (2, 768, 128), (8, 128), (768, 128), (12, 128, 512), (384, 128)]
    held_big, held_small = 128, 384
    plan_big, plan_small = reduce_plan(dp_bits, 128), reduce_plan(dp_bits, 384)
    for index in range(len(dp_bits)):
        held_big = plan_big[index][1] or held_big
        held_small = plan_small[index][1] or held_small
        landing += [(12, held_big, 512), (held_small, 128)]
    vmem = pltpu.VMEM
    dma = pltpu.SemaphoreType.DMA
    steps = 5 + 2 * len(dp_bits)
    return pl.pallas_call(
        functools.partial(mega_kernel, dp_bits, len(landing)),
        out_shape=(
            jax.ShapeDtypeStruct((12, 2, 128, 512), b16),
            jax.ShapeDtypeStruct((768, 128), b16),
            jax.ShapeDtypeStruct((8, 128), f32),
        ),
        in_specs=[pl.BlockSpec(memory_space=pltpu.VMEM)]
        + [pl.BlockSpec(memory_space=pl.ANY)] * 4
        + [pl.BlockSpec(memory_space=pltpu.VMEM)] * 5,
        out_specs=[pl.BlockSpec(memory_space=pltpu.VMEM)] * 3,
        scratch_shapes=[
            vmem((keep, 2 * rows.shape[1], 128), f32),
            vmem((768, 512), b16),
            vmem((2, 8, 2, 2, 128, 512), b16),
            vmem((2, 2, 2, 4, 128, 512), b16),
            vmem((2, number, 512), f32),
            vmem((2, number, 512), f32),
            vmem((2, 3, number, 512), b16),
            vmem((2, pairs, 2, 512), f32),
            vmem((2, number, 512), b16),
            vmem((2, 4, number, 512), b16),
            vmem((number, 512), f32),
            vmem((4, number, 512), b16),
            vmem((number, 512), b16),
            vmem((number, 512), b16),
            vmem((number, 512), b16),
            vmem((number, 512), b16),
            vmem((128, 512), f32),
            vmem((16, 512), f32),
            vmem((2, 2, 768, 128), b16),
            vmem((2 * levels + 1, 8, 128), f32),
        ]
        + [vmem(shape, b16) for shape in landing]
        + [
            dma((9, 5)),
            dma((9, 5)),
            dma((2, 9)),
            dma((2,)),
            dma((1,)),
            dma((13, steps)),
            dma((13, steps)),
            dma((levels,)),
            dma((levels,)),
            pltpu.SemaphoreType.REGULAR((2,)),
            pltpu.SemaphoreType.REGULAR((2,)),
        ],
        compiler_params=pltpu.CompilerParams(
            collective_id=0, has_side_effects=True, vmem_limit_bytes=VMEM_LIMIT
        ),
    )(rows, *weights, *smalls)


def advance(weight, gradient, momentum, average, step_rate):
    new_momentum = MOMENTUM_KEEP * momentum + gradient
    new_weight = weight - step_rate * (gradient + MOMENTUM_KEEP * new_momentum)
    new_average = AVERAGE_KEEP * average + (1.0 - AVERAGE_KEEP) * new_weight
    return (new_weight, new_momentum, new_average)


def update_kernel(step_rate, wide_grad, tall_grad, small_grad, sums, *refs):
    inputs, outputs = refs[:27], refs[27:]
    scale = 1.0 / sums[0:1, 1:2]

    def put(member, place, gradient):
        entry = [inputs[9 * part + member][place] for part in range(3)]
        results = advance(entry[0], wide(gradient) * scale, entry[1], entry[2], step_rate)
        for part in range(3):
            outputs[9 * part + member][place] = results[part]

    places = (8, 9, 10, 11, 0, 1, 2, 3)
    for j in range(8):
        member = 0 if j < 3 else (1 if j == 3 else 2)
        column = 512 * (j if j < 3 else (0 if j == 3 else j - 4))
        gradient = wide_grad[0, places[j] if j < 4 else j - 4]
        put(member, (0, slice(None), slice(column, column + 512)), gradient)
    put(3, (0,), tall_grad[0, 0])

    @pl.when((pl.program_id(0) == 0) & (pl.program_id(1) == 0))
    def _():
        put(4, (...,), small_grad[640:648])
        put(5, (...,), small_grad[0:64])
        put(6, (...,), small_grad[64:128])
        put(7, (...,), small_grad[128:640])
        put(8, (...,), small_grad[648:650])


def update_call(big, small, sums, params, moments, averages, step_rate):
    big = big.reshape(2, 12, 128, 512)

    def block(rows, columns):
        return pl.BlockSpec((1, rows, columns), lambda l, i: (l, i, 0))

    def whole(*shape):
        return pl.BlockSpec(shape, lambda l, i: (0,) * len(shape))

    one_set = [
        block(32, 1536),
        block(32, 512),
        block(32, 2048),
        block(128, 512),
        whole(8, 128),
        whole(64, 128),
        whole(64, 128),
        whole(512, 128),
        whole(2, 128),
    ]
    arrays = []
    for group in (params, moments, averages):
        group = list(group)
        group[4] = group[4].reshape(8, 128)
        arrays += group
    out = pl.pallas_call(
        functools.partial(update_kernel, step_rate),
        grid=(2, 4),
        out_shape=[jax.ShapeDtypeStruct(array.shape, jnp.float32) for array in arrays],
        in_specs=[
            pl.BlockSpec((1, 12, 32, 512), lambda l, i: (1 - l, 0, i, 0)),
            pl.BlockSpec((1, 1, 128, 512), lambda l, i: (1 - l, 4 + i, 0, 0)),
            whole(768, 128),
            whole(8, 128),
        ]
        + one_set * 3,
        out_specs=one_set * 3,
        compiler_params=pltpu.CompilerParams(vmem_limit_bytes=VMEM_LIMIT),
    )(big, big, small, sums, *arrays)
    out = list(out)
    for part in range(3):
        out[9 * part + 4] = out[9 * part + 4].reshape(2, 4, 128)
    return out


def per_device(series_data, patch_mask, *state):
    params, moments, averages = state[:9], state[9:18], state[18:]
    total_series = series_data.shape[0] * lax.axis_size("dp") * lax.axis_size("fsdp")
    step_rate = RATE_FACTOR * math.sqrt(total_series * PATCHES)
    series_num, local_count = patch_mask.shape
    patches = series_data.reshape(series_num, local_count, PATCH)
    masked = jnp.broadcast_to(patch_mask.astype(jnp.float32)[..., None], patches.shape)
    rows = jnp.concatenate([patches, masked], axis=-1)
    qkv, out, up, down, norms, embed_w, head, pos, final = params
    big, small, sums = mega_call(
        rows,
        (qkv, out, up, down),
        (embed_w, head, pos, norms.reshape(8, 128), final),
        lax.axis_size("dp"),
    )
    new = update_call(big, small, sums, params, moments, averages, step_rate)
    return (sums[0, 0], sums[0, 1], *new)


def solution(mesh):
    matrix_spec = P(None, "fsdp", None)
    column = P(None, "fsdp")
    one_set = (matrix_spec,) * 4 + (P(None, None, "fsdp"),) + (column,) * 4
    data = P(("dp", "fsdp"), "seq")
    return jax.shard_map(
        per_device,
        mesh=mesh,
        in_specs=(data, data) + one_set * 3,
        out_specs=(P(), P()) + one_set * 3,
        check_vma=False,
    )
```

```python
import functools
import math

import jax
import jax.numpy as jnp
from jax import lax
from jax.experimental import pallas as pl
from jax.experimental.pallas import tpu as pltpu
from jax.sharding import PartitionSpec as P

D = 512
HEADS = 8
HEAD_DIM = 64
PATCH = 64
PATCHES = 512
LAYERS = 2
NORM_EPS = 1e-05
SCORE_SCALE = 0.125
MOMENTUM_KEEP = 0.9
AVERAGE_KEEP = 0.9
RATE_FACTOR = 0.5
MESH = pl.DeviceIdType.MESH
VMEM_LIMIT = 63 * 2**20


def flip(index, bit):
    return index + bit - 2 * bit * ((index // bit) % 2)


def position():
    return lax.axis_index("dp"), lax.axis_index("seq"), lax.axis_index("fsdp")


def bits_of(extent):
    found = []
    bit = 1
    while bit < extent:
        found.append(bit)
        bit *= 2
    return found


def greet(partners):
    barrier = pltpu.get_barrier_semaphore()
    for partner in partners:
        pl.semaphore_signal(barrier, inc=1, device_id=partner, device_id_type=MESH)
    pl.semaphore_wait(barrier, len(partners))


def remote(src, dst, send_sem, recv_sem, partner):
    return pltpu.make_async_remote_copy(
        src_ref=src,
        dst_ref=dst,
        send_sem=send_sem,
        recv_sem=recv_sem,
        device_id=partner,
        device_id_type=MESH,
    )

RB = 512
SERIES_ROWS = 512
GELU_A = math.sqrt(2.0 / math.pi)
GELU_B = 0.044715


def dot_nn(left, right):
    return jnp.dot(left, right, preferred_element_type=jnp.float32)


def dot_nt(left, right):
    return lax.dot_general(left, right, (((1,), (1,)), ((), ())), preferred_element_type=jnp.float32)


def dot_tn(left, right):
    return lax.dot_general(left, right, (((0,), (0,)), ((), ())), preferred_element_type=jnp.float32)


def low(value):
    return value.astype(jnp.bfloat16)


def wide(value):
    return value.astype(jnp.float32)


def normalise(rows):
    centred = rows - jnp.mean(rows, axis=-1, keepdims=True)
    variance = jnp.mean(centred * centred, axis=-1, keepdims=True)
    inverse = lax.rsqrt(variance + NORM_EPS)
    return centred * inverse, inverse


def norm_back(grad_rows, scaled, inverse, gain):
    inner = grad_rows * gain
    first = jnp.mean(inner, axis=-1, keepdims=True)
    second = jnp.mean(inner * scaled, axis=-1, keepdims=True)
    return inverse * (inner - first - scaled * second)


def column_sum(value):
    return jnp.sum(value, axis=0, keepdims=True)


def matrix(square, l, j):
    return square[l, j].reshape(512, 512)


def row_block(index, size=RB):
    return pl.ds(pl.multiple_of(index * size, size), size)


def forward_in(l, refs, hook):
    small, square, tall, hid, mid, qkv, lse, ctx, up = refs
    gain, bias = wide(small[640 + 4 * l : 641 + 4 * l]), wide(small[641 + 4 * l : 642 + 4 * l])

    def body(i, carry):
        r = row_block(i)
        normed = low(normalise(hid[l, r])[0] * gain + bias)
        for j in range(3):
            got = dot_nn(normed, matrix(square, l, j))
            if j == 0:
                got = got * SCORE_SCALE
            qkv[l, j, r] = low(got)
        return carry

    split_loop(body, hid.shape[1] // RB, 2, hook, 2.4)


def pair_slices(index):
    series, pair = index // 4, index % 4
    return row_block(series, SERIES_ROWS), pl.ds(pl.multiple_of(128 * pair, 128), 128)


def head_mask(block, head):
    lane = lax.broadcasted_iota(jnp.int32, block.shape, 1)
    keep = lane < HEAD_DIM if head == 0 else lane >= HEAD_DIM
    return jnp.where(keep, block, jnp.zeros_like(block))


def forward_attention(l, refs, hook):
    small, square, tall, hid, mid, qkv, lse, ctx, up = refs

    def body(step, carry):
        loaded = []
        for sub in range(2):
            r, columns = pair_slices(2 * step + sub)
            loaded.append([qkv[l, part, r, columns] for part in range(3)])
        order = [(sub, head) for sub in range(2) for head in range(2)]
        scores = {}

        def ask(at):
            if at < len(order):
                sub, head = order[at]
                query, key, value = loaded[sub]
                scores[at] = dot_nt(head_mask(key, head), query)

        for at in range(2):
            ask(at)
        parts = []
        for at, (sub, head) in enumerate(order):
            ask(at + 2)
            index = 2 * step + sub
            r, columns = pair_slices(index)
            found = scores.pop(at)
            value_t = loaded[sub][2].T
            top = jnp.max(found, axis=0, keepdims=True)
            weights = jnp.exp(found - top)
            total = column_sum(weights)
            lse[l, index, head : head + 1] = top + jnp.log(total)
            part = dot_nn(value_t[64 * head : 64 * head + 64], low(weights))
            parts.append(part * (1.0 / total))
            if head == 1:
                ctx[l, r, columns] = low(jnp.concatenate(parts, axis=0).T)
                parts = []
        return carry

    split_loop(body, lse.shape[1] // 2, 8 // 2, hook, 6.9)


def forward_out(l, refs, target, hook):
    small, square, tall, hid, mid, qkv, lse, ctx, up = refs
    gain, bias = wide(small[642 + 4 * l : 643 + 4 * l]), wide(small[643 + 4 * l : 644 + 4 * l])

    def body(i, carry):
        r = row_block(i, 512)
        middle = hid[l, r] + dot_nn(ctx[l, r], matrix(square, l, 3))
        mid[l, r] = middle
        normed = low(normalise(middle)[0] * gain + bias)
        result = middle
        raises = [dot_nn(normed, matrix(square, l, 4 + j)) for j in range(1)]
        for j in range(4):
            if j + 1 < 4:
                raises.append(dot_nn(normed, matrix(square, l, 4 + j + 1)))
            raised = raises[j]
            up[l, j, r] = low(raised)
            bend = jnp.tanh(raised * (GELU_A + (GELU_A * GELU_B) * raised * raised))
            halved = 0.5 * raised
            active = low(halved + halved * bend)
            result = result + dot_nn(active, tall[l, j // 2, j % 2].reshape(512, 512))
        target[r] = result
        return carry

    split_loop(body, hid.shape[1] // 512, 2, hook, 6.1)


def masked_input(block):
    lane = lax.broadcasted_iota(jnp.int32, block.shape, 1)
    hidden = block * (1.0 - pltpu.roll(block, 64, 1))
    return low(jnp.where(lane < PATCH, hidden, 0.0))


def split_loop(body, count, parts, hook, cost):
    size = count // parts
    for part in range(parts):
        lax.fori_loop(part * size, (part + 1) * size, body, 0)
        hook(cost / parts)


def embed(rows, small, hid):
    def body(i, carry):
        r = row_block(i)
        place = pl.ds(pl.multiple_of(128 + (i * RB) % PATCHES, 128), RB)
        hid[0, r] = dot_nn(masked_input(rows[r]), small[0:128]) + wide(small[place])
        return carry

    lax.fori_loop(0, hid.shape[1] // RB, body, 0)


def top(rows, small, grad, head_grad, norm_grad, sums):
    gain, bias = wide(small[648:649]), wide(small[649:650])
    head_grad[...] = jnp.zeros_like(head_grad)

    def body(i, carry):
        loss, count, gain_sum, bias_sum = carry
        r = row_block(i)
        block = rows[r]
        lane = lax.broadcasted_iota(jnp.int32, block.shape, 1)
        mask = jnp.where(lane >= PATCH, block, 0.0)
        scaled, inverse = normalise(grad[r])
        final = low(scaled * gain + bias)
        errors = dot_nt(final, small[0:128]) - pltpu.roll(block, 64, 1)
        wrong = errors * mask
        pull = low(2.0 * wrong)
        head_grad[...] += dot_tn(pull, final)
        below = dot_nn(pull, small[0:128])
        grad[r] = norm_back(below, scaled, inverse, gain)
        return (
            loss + column_sum(errors * wrong),
            count + column_sum(mask),
            gain_sum + column_sum(below * scaled),
            bias_sum + column_sum(below),
        )

    zero, line = jnp.zeros((1, 512), jnp.float32), jnp.zeros((1, 128), jnp.float32)
    loss, count, gain_sum, bias_sum = lax.fori_loop(
        0, grad.shape[0] // RB, body, (line, line, zero, zero)
    )
    norm_grad[8:9] = gain_sum
    norm_grad[9:10] = bias_sum
    lane = lax.broadcasted_iota(jnp.int32, (8, 128), 1)
    sums[...] = jnp.where(lane == 0, jnp.sum(loss), jnp.where(lane == 1, jnp.sum(count), 0.0))


def backward_mlp(l, refs, grad, act, back16, normed16, dctx, norm_grad, hook):
    small, square, tall, hid, mid, qkv, lse, ctx, up = refs
    gain, bias = wide(small[642 + 4 * l : 643 + 4 * l]), wide(small[643 + 4 * l : 644 + 4 * l])

    def body(i, carry):
        r = row_block(i)
        upstream = grad[r]
        upstream16 = low(upstream)
        back16[r] = upstream16
        below = jnp.zeros((RB, 512), jnp.float32)

        def pull(j):
            return dot_nt(upstream16, tall[l, j // 2, j % 2].reshape(512, 512))

        pulls = [pull(0), pull(1)]
        for j in range(4):
            if j < 2:
                pulls.append(pull(j + 2))
            pulled = wide(low(pulls[j]))
            raised = wide(up[l, j, r])
            square_u = raised * raised
            bend = jnp.tanh(raised * (GELU_A + (GELU_A * GELU_B) * square_u))
            half = 0.5 + 0.5 * bend
            act[j, r] = low(raised * half)
            slope = half + (raised * (0.5 * GELU_A + (1.5 * GELU_A * GELU_B) * square_u)) * (
                1.0 - bend * bend
            )
            inner = low(pulled * slope)
            up[l, j, r] = inner
            below = below + dot_nt(inner, matrix(square, l, 4 + j))
        scaled, inverse = normalise(mid[l, r])
        middle = upstream + norm_back(below, scaled, inverse, gain)
        grad[r] = middle
        normed16[r] = low(scaled * gain + bias)
        dctx[r] = low(dot_nt(low(middle), matrix(square, l, 3)))
        norm_grad[4 * l + 2 : 4 * l + 3] += column_sum(below * scaled)
        norm_grad[4 * l + 3 : 4 * l + 4] += column_sum(below)
        return carry

    split_loop(body, grad.shape[0] // RB, 2, hook, 7.5)


def weights_mlp(l, refs, grad, act, back16, normed16, ready, allow, hook):
    small, square, tall, hid, mid, qkv, lse, ctx, up = refs
    square[l, 3] = low(dot_tn(ctx[l], low(grad[...]))).reshape(2, 2, 128, 512)
    for j in range(4):
        tile = low(dot_tn(normed16[...], up[l, j]))
        square[l, 4 + j] = tile.reshape(2, 2, 128, 512)
    ready()
    allow(2)
    hook(2.9)
    for j in range(4):
        tile = low(dot_tn(act[j], back16[...]))
        tall[l, j // 2, j % 2] = tile.reshape(4, 128, 512)
        if j == 1:
            hook(1.15)
    allow(4)
    hook(1.15)


def backward_attention(l, refs, dctx, hook):
    small, square, tall, hid, mid, qkv, lse, ctx, up = refs

    def body(step, carry):
        loaded = []
        for sub in range(1):
            r, columns = pair_slices(1 * step + sub)
            loaded.append([qkv[l, part, r, columns] for part in range(3)] + [dctx[r, columns]])
        order = [(sub, head) for sub in range(1) for head in range(2)]
        products = {}

        def ask(at):
            if at < len(order):
                sub, head = order[at]
                query, key, value, pulled = loaded[sub]
                products[at] = (
                    dot_nt(head_mask(key, head), query),
                    dot_nt(head_mask(value, head), pulled),
                )

        for at in range(1):
            ask(at)
        queries_t, keys, values = [], [], []
        for at, (sub, head) in enumerate(order):
            ask(at + 1)
            index = 1 * step + sub
            query, key, value, pulled = loaded[sub]
            key_t = key.T
            scores, grad_weights = products.pop(at)
            weights = jnp.exp(scores - lse[l, index, head : head + 1])
            inner = weights * grad_weights
            grad_scores = low(inner - weights * column_sum(inner))
            values.append(dot_nn(low(weights), pulled))
            keys.append(dot_nn(grad_scores, query))
            queries_t.append(dot_nn(key_t[64 * head : 64 * head + 64], grad_scores))
            if head == 1:
                r, columns = pair_slices(index)
                lane = lax.broadcasted_iota(jnp.int32, (SERIES_ROWS, 128), 1)
                qkv[l, 0, r, columns] = low(jnp.concatenate(queries_t, axis=0).T * SCORE_SCALE)
                qkv[l, 1, r, columns] = low(jnp.where(lane < HEAD_DIM, keys[0], keys[1]))
                qkv[l, 2, r, columns] = low(jnp.where(lane < HEAD_DIM, values[0], values[1]))
                queries_t, keys, values = [], [], []
        return carry

    split_loop(body, lse.shape[1] // 1, 8, hook, 12.2)


def backward_in(l, refs, grad, normed16, norm_grad, hook):
    small, square, tall, hid, mid, qkv, lse, ctx, up = refs
    gain, bias = wide(small[640 + 4 * l : 641 + 4 * l]), wide(small[641 + 4 * l : 642 + 4 * l])

    def body(i, carry):
        r = row_block(i)
        below = dot_nt(qkv[l, 0, r], matrix(square, l, 0))
        for j in range(1, 3):
            below = below + dot_nt(qkv[l, j, r], matrix(square, l, j))
        scaled, inverse = normalise(hid[l, r])
        grad[r] = grad[r] + norm_back(below, scaled, inverse, gain)
        normed16[r] = low(scaled * gain + bias)
        norm_grad[4 * l : 4 * l + 1] += column_sum(below * scaled)
        norm_grad[4 * l + 1 : 4 * l + 2] += column_sum(below)
        return carry

    split_loop(body, grad.shape[0] // RB, 2, hook, 2.4)


def weights_in(l, refs, normed16):
    square, qkv = refs[1], refs[5]
    for j in range(3):
        square[l, j] = low(dot_tn(normed16[...], qkv[l, j])).reshape(2, 2, 128, 512)


def small_grads(rows, grad, head_grad, norm_grad, store):
    def put(first, block):
        for owner in range(4):
            store[owner // 2, owner % 2, first : first + block.shape[0]] = low(
                block[:, 128 * owner : 128 * owner + 128]
            )

    total = head_grad[...]
    for i in range(rows.shape[0] // 512):
        r = slice(512 * i, 512 * i + 512)
        total = total + dot_tn(masked_input(rows[r]), low(grad[r]))
    put(0, total)
    summed = grad[0:512]
    for i in range(1, rows.shape[0] // 512):
        summed = summed + grad[512 * i : 512 * i + 512]
    put(128, summed)
    put(640, norm_grad[...])
    for owner in range(4):
        store[owner // 2, owner % 2, 656:768] = jnp.zeros((112, 128), jnp.bfloat16)


class Clock:
    RATES = {"core": 440e3, "y": 45e3, "x": 45e3, "z1": 45e3, "z2": 22.5e3}

    def __init__(self):
        self.now = 0.0
        self.free = dict.fromkeys(self.RATES, 0.0)

    def send(self, link, size):
        self.free[link] = max(self.free[link], self.now) + size / self.RATES[link]
        return self.free[link] + 2.2

    def reach(self, moment):
        self.now = max(self.now, moment)


def run_gather(clock, position_now, weights, smalls, square, tall, small, stage, sems):
    dp, seq, high, low_bit = position_now
    fsdp = 2 * high + low_bit
    send_sem, recv_sem, stage_sem = sems
    core = (dp, seq, 2 * high + 1 - low_bit)
    other = (dp, seq, 2 * (1 - high) + low_bit)
    twin = (dp, 1 - seq, fsdp)
    qkv_w, out_w, up_w, down_w = weights

    def lanes(owner):
        return pl.ds(pl.multiple_of(128 * owner, 128), 128)

    def small_full(y, c):
        return small.at[:, lanes(2 * y + c)]

    def small_part(y, c, half):
        return small.at[pl.ds(pl.multiple_of(384 * half, 128), 384), lanes(2 * y + c)]

    places = [(small_full, small_part)]
    for l in range(LAYERS):
        for first, number in ((0, 1), (1, 1), (2, 1), (3, 1), (4, 4)):
            places.append(
                (
                    lambda y, c, l=l, js=pl.ds(first, number): square.at[l, js, y, c],
                    lambda y, c, half, l=l, js=pl.ds(first, number): square.at[
                        l, js, y, c, pl.ds(pl.multiple_of(64 * half, 64), 64)
                    ],
                )
            )
        places.append(
            (
                lambda y, c, l=l: tall.at[l, y, c],
                lambda y, c, half, l=l: tall.at[l, y, c, pl.ds(2 * half, 2)],
            )
        )

    def copies(number):
        full, part = places[number]
        near, far = (high, low_bit), (1 - high, low_bit)
        moves = [
            (full(*near), core),
            (part(*near, seq), other),
            (part(*far, seq), twin),
            (part(*far, seq), core),
            (part(*far, 1 - seq), core),
        ]
        return [
            remote(ref, ref, send_sem.at[number, kind], recv_sem.at[number, kind], partner)
            for kind, (ref, partner) in enumerate(moves)
        ]

    every = [copies(number) for number in range(len(places))]

    staged = []
    for l in range(LAYERS):
        moves = [(qkv_w.at[l, :, pl.ds(512 * j, 512)], j, 1) for j in range(3)]
        moves += [(out_w.at[l], 3, 1)]
        moves += [(up_w.at[l, :, pl.ds(512 * j, 512)], 4 + j, 1) for j in range(4)]
        moves += [(down_w.at[l], 8, 4)]
        for index, (src, first, number) in enumerate(moves):
            dst = stage(l, first, number)
            copy = pltpu.make_async_copy(src, dst, stage_sem.at[l, index])
            copy.start()
            staged.append((copy, l, first, number, dst))

    embed_w, head_w, pos_w, norms_w, final_w = smalls
    mine = lanes(fsdp)
    small[0:64, mine] = low(embed_w[...])
    small[64:128, mine] = low(head_w[...])
    small[128:640, mine] = low(pos_w[...])
    small[640:656, mine] = low(jnp.concatenate([norms_w[...], final_w[...], jnp.zeros((6, 128))]))
    small[656:768, mine] = jnp.zeros((112, 128), jnp.bfloat16)

    def size(number):
        full = places[number][0](0, 0)
        return 2 * math.prod(full.shape)

    waiting = {}

    def launch(number):
        every[number][1].start()
        every[number][0].start()
        waiting[(1, number)] = clock.send("y", size(number) / 2)

    def launch_rest():
        ends = {0: 1, 1: 2, 2: 3, 3: 4, 7: 5, 8: 6}
        for copy, l, first, number, dst in staged:
            copy.wait()
            if first < 8:
                square[l, first, high, low_bit] = low(dst[...])
            else:
                tall[l, high, low_bit] = low(dst[...]).reshape(4, 128, 512)
            if first in ends:
                launch(6 * l + ends[first])

    def arrive(kind, number):
        clock.reach(waiting.pop((kind, number)))
        every[number][kind].wait_recv()
        if kind == 1:
            every[number][2].start()
            waiting[(2, number)] = clock.send("x", size(number) / 2)
            every[number][3].start()
        else:
            every[number][4].start()

    def soonest():
        return min(waiting, key=lambda entry: (waiting[entry], entry))

    def pump():
        while waiting and waiting[soonest()] <= clock.now:
            arrive(*soonest())

    def finish(number):
        while (1, number) in waiting or (2, number) in waiting:
            arrive(*soonest())
        for kind in (0, 3, 4):
            every[number][kind].wait_recv()

    def close():
        for entry in every:
            for copy in entry:
                copy.wait_send()

    return launch, launch_rest, pump, finish, close


def run_reduce(clock, position_now, dp_bits, buffers, ready, sems):
    dp, seq, high, low_bit = position_now
    fsdp = 2 * high + low_bit
    core = (dp, seq, 2 * high + 1 - low_bit)
    other = (dp, seq, 2 * (1 - high) + low_bit)
    twin = (dp, 1 - seq, fsdp)
    lines = [(flip(dp, bit), seq, fsdp) for bit in dp_bits]
    square, tall, up, qkv, ctx, small_store, landing, out_big, out_small = buffers
    ready_core, ready_other, ready_twin = ready
    send_sem, recv_sem = sems
    first_land = up.reshape(2, 8, 2, 2, 128, 512)
    second_land = qkv.reshape(2, 12, 2, 128, 512)
    early_land = ctx.reshape(2, 4, 2, 128, 512)
    third_land = up.reshape(2, 32, 128, 512)

    def describe(n):
        if n == 12:
            small_land = landing[1::2]
            return dict(
                source=lambda lane: small_store.at[:, lane],
                land=[small_land[0], small_land[1]] + list(small_land[2:]),
                of_y=lambda ref, y: ref.at[y],
                half=lambda ref, s: ref.at[pl.ds(pl.multiple_of(384 * s, 128), 384)],
                final=out_small,
                rows=384,
            )
        l, k = 1 - n // 6, n % 6
        if k in (2, 3):
            source = lambda lane: tall.at[l, :, lane, pl.ds(2 * (k - 2), 2)]
            of_y = lambda ref, y: ref.at[y]
        else:
            first = (4, 6, None, None, 0, 2)[k]
            source = lambda lane: square.at[l, pl.ds(first, 2), :, lane]
            of_y = lambda ref, y: ref.at[:, y]
        second = early_land.at[1, n] if n < 4 else second_land.at[1, n - 4]
        return dict(
            source=source,
            land=[first_land.at[l, k], second, third_land.at[l, 24 + k]]
            + [ref.at[n] for ref in landing[6::2]],
            of_y=of_y,
            half=lambda ref, s: ref.at[s],
            final=out_big.at[n],
            rows=128,
        )

    chunks = [describe(n) for n in range(13)]
    pending, started, due = {}, [], {}

    def begin(n, step, src, dst, partner, link):
        copy = remote(src, dst, send_sem.at[n, step], recv_sem.at[n, step], partner)
        copy.start()
        started.append(copy)
        pending[n] = copy
        due[n] = clock.send(link, 2 * math.prod(src.shape))

    def advance_chunk(n, step):
        chunk = chunks[n]
        land = chunk["land"]
        plan = reduce_plan(dp_bits, chunk["rows"])
        if step > 0:
            pending.pop(n).wait_recv()
        if step == 0:
            if n in (0, 6):
                pl.semaphore_wait(ready_core.at[n // 6], 1)
            begin(n, step, chunk["source"](1 - low_bit), land[0], core, "core")
            return
        if step == 1:
            land[0][...] += chunk["source"](low_bit)[...]
            if n in (0, 4):
                pl.semaphore_wait(ready_other.at[n // 4], 1)
            begin(n, step, chunk["of_y"](land[0], 1 - high), land[1], other, "y")
            return
        if step == 2:
            land[1][...] += chunk["of_y"](land[0], high)[...]
            if n in (0, 6):
                pl.semaphore_wait(ready_twin.at[n // 6], 1)
            begin(n, step, chunk["half"](land[1], 1 - seq), land[2], twin, "x")
            return
        if step == 3:
            land[2][...] += chunk["half"](land[1], seq)[...]
        at = step - 3
        offset, starts = 0, []
        for bit, kept in plan:
            side = (dp // bit) % 2
            starts.append(offset + side * kept)
            offset = offset + side * kept
        final = chunk["half"](chunk["final"], seq)
        if at <= len(plan):
            if at > 0:
                bit, kept = plan[at - 1]
                previous = land[1 + at]
                if kept:
                    side = (dp // bit) % 2
                    previous = previous.at[pl.ds(pl.multiple_of(side * kept, 16), kept)]
                land[2 + at][...] += previous[...]
            held = land[2 + at]
            if at < len(plan):
                bit, kept = plan[at]
                src = held
                if kept:
                    side = (dp // bit) % 2
                    src = held.at[pl.ds(pl.multiple_of((1 - side) * kept, 16), kept)]
                begin(n, step, src, land[3 + at], lines[at], "z%d" % min(plan[at][0], 2))
                return
            final[pl.ds(pl.multiple_of(offset, 16), held.shape[0])] = held[...]
        back = [index for index in range(len(plan)) if plan[index][1]][::-1]
        turn = at - len(plan)
        if turn < len(back):
            index = back[turn]
            piece = final.at[pl.ds(pl.multiple_of(starts[index], 16), plan[index][1])]
            begin(n, step, piece, piece, lines[index], "z%d" % min(plan[index][0], 2))
        elif turn == len(back):
            begin(n, step, final, final, twin, "x")

    progress = [0] * 13
    last = []
    for chunk in chunks:
        plan = reduce_plan(dp_bits, chunk["rows"])
        last.append(4 + len(plan) + sum(1 for entry in plan if entry[1]))
    allowed = [0]

    def move(n):
        clock.reach(due.pop(n, 0.0))
        advance_chunk(n, progress[n])
        clock.now += 0.2
        progress[n] += 1

    def open_chunks():
        return [n for n in range(allowed[0]) if progress[n] <= last[n]]

    def soonest():
        return min(open_chunks(), key=lambda n: (due.get(n, 0.0), n))

    def tick():
        while open_chunks() and due.get(soonest(), 0.0) <= clock.now:
            move(soonest())

    def allow(count):
        allowed[0] = count

    def drain():
        while open_chunks():
            move(soonest())
        for copy in started:
            copy.wait_send()

    def ready_for(partner, semaphore):
        pl.semaphore_signal(semaphore, inc=1, device_id=partner, device_id_type=MESH)

    def up_free(i):
        ready_for(core, ready_core.at[i])
        ready_for(twin, ready_twin.at[i])

    return tick, allow, drain, up_free, lambda i: ready_for(other, ready_other.at[i])


def reduce_plan(dp_bits, rows):
    plan = []
    for bit in dp_bits:
        if rows % 32 == 0:
            rows //= 2
            plan.append((bit, rows))
        else:
            plan.append((bit, 0))
    return plan


def mega_kernel(dp_bits, landings, *refs):
    rows_in, qkv_w, out_w, up_w, down_w, embed_w, head_w, pos_w, norms_w, final_w = refs[:10]
    out_big, out_small, out_sums = refs[10:13]
    (rows, small, square, tall, hid, mid, qkv, lse, ctx, up, grad, act, back16, normed16, dctx,
     head_grad, norm_grad, small_store, loss_land) = refs[13:32]
    landing = refs[32 : 32 + landings]
    (gather_send, gather_recv, stage_sem, rows_sem, rows_local, reduce_send, reduce_recv, loss_send,
     loss_recv, ready_core, ready_other, ready_twin) = refs[32 + landings :]
    dp, seq, fsdp = position()
    high, low_bit = fsdp // 2, fsdp % 2
    place = (dp, seq, high, low_bit)
    core = (dp, seq, 2 * high + 1 - low_bit)
    other = (dp, seq, 2 * (1 - high) + low_bit)
    twin = (dp, 1 - seq, fsdp)
    partners = [core, other, twin] + [(flip(dp, bit), seq, fsdp) for bit in dp_bits]

    def stage(l, first, number):
        if first < 8:
            return mid.at[l, pl.ds(128 * first, 128 * number)]
        return (hid.at[1] if l == 0 else grad).at[pl.ds(0, 512)]

    clock = Clock()
    launch, launch_rest, pump, finish, close = run_gather(
        clock,
        place,
        (qkv_w, out_w, up_w, down_w),
        (embed_w, head_w, pos_w, norms_w, final_w),
        square,
        tall,
        small,
        stage,
        (gather_send, gather_recv, stage_sem),
    )
    greet(partners)
    launch(0)
    keep, local = rows_in.shape[0] // 2, rows_in.shape[1]
    mine = rows.at[:, pl.ds(pl.multiple_of(local * seq, local), local)]
    trade = remote(
        rows_in.at[pl.ds(keep * (1 - seq), keep)], mine, rows_sem.at[0], rows_sem.at[1], twin
    )
    trade.start()
    traded = clock.send("x", 4 * math.prod(rows_in.shape) // 2)
    own = pltpu.make_async_copy(rows_in.at[pl.ds(keep * seq, keep)], mine, rows_local.at[0])
    own.start()
    launch_rest()
    norm_grad[...] = jnp.zeros_like(norm_grad)
    finish(0)
    own.wait()
    trade.wait()
    clock.reach(traded)

    parts = (small, square, tall, hid, mid, qkv, lse, ctx, up)
    flat_rows = rows.reshape(rows.shape[0] * rows.shape[1], 128)
    def pump_after(cost):
        clock.now += cost
        pump()

    embed(flat_rows, small, hid)
    pump_after(1.2)
    for l in range(LAYERS):
        for number in range(6 * l + 1, 6 * l + 4):
            finish(number)
        forward_in(l, parts, pump_after)
        forward_attention(l, parts, pump_after)
        for number in range(6 * l + 4, 6 * l + 7):
            finish(number)
        forward_out(l, parts, hid.at[1] if l == 0 else grad, pump_after)
    close()
    top(flat_rows, small, grad, head_grad, norm_grad, loss_land.at[0])
    clock.now += 2.6

    tick, allow, drain, ready_to_core, ready_to_other = run_reduce(
        clock,
        place,
        dp_bits,
        (square, tall, up, qkv, ctx, small_store, landing, out_big, out_small),
        (ready_core, ready_other, ready_twin),
        (reduce_send, reduce_recv),
    )
    loss_state = {}
    loss_step = [0]

    def loss_tick():
        step = loss_step[0]
        if step > len(partners):
            return
        loss_step[0] += 1
        if step > 0:
            loss_state[step - 1].wait_recv()
            loss_land[2 * step] = loss_land[2 * step - 2] + loss_land[2 * step - 1]
        if step < len(partners):
            loss_state[step] = remote(
                loss_land.at[2 * step],
                loss_land.at[2 * step + 1],
                loss_send.at[step],
                loss_recv.at[step],
                partners[step],
            )
            loss_state[step].start()
        else:
            out_sums[...] = loss_land[2 * step]

    def hook(cost):
        clock.now += cost
        tick()
        loss_tick()

    for l in reversed(range(LAYERS)):
        before = 0 if l == 1 else 6
        backward_mlp(l, parts, grad, act, back16, normed16, dctx, norm_grad, hook)

        def ready():
            ready_to_core(1 - l)
            if l == 1:
                ready_to_other(0)

        weights_mlp(
            l, parts, grad, act, back16, normed16, ready, lambda k: allow(before + k), hook
        )
        backward_attention(l, parts, dctx, hook)
        backward_in(l, parts, grad, normed16, norm_grad, hook)
        weights_in(l, parts, normed16)
        if l == 1:
            ready_to_other(1)
        allow(before + 6)
        hook(2.0)
    small_grads(flat_rows, grad, head_grad, norm_grad, small_store)
    clock.now += 0.7
    allow(13)
    while loss_step[0] <= len(partners):
        loss_tick()
    drain()
    for copy in loss_state.values():
        copy.wait_send()


def mega_call(rows, weights, smalls, dp_extent):
    dp_bits = bits_of(dp_extent)
    levels = 3 + len(dp_bits)
    number = rows.shape[0] * rows.shape[1]
    keep = rows.shape[0] // 2
    pairs = keep * 4
    f32, b16 = jnp.float32, jnp.bfloat16
    landing = [(8, 128), (2, 768, 128), (8, 128), (768, 128), (8, 128), (384, 128)]
    held_big, held_small = 128, 384
    plan_big, plan_small = reduce_plan(dp_bits, 128), reduce_plan(dp_bits, 384)
    for index in range(len(dp_bits)):
        held_big = plan_big[index][1] or held_big
        held_small = plan_small[index][1] or held_small
        landing += [(12, held_big, 512), (held_small, 128)]
    vmem = pltpu.VMEM
    dma = pltpu.SemaphoreType.DMA
    steps = 5 + 2 * len(dp_bits)
    return pl.pallas_call(
        functools.partial(mega_kernel, dp_bits, len(landing)),
        out_shape=(
            jax.ShapeDtypeStruct((12, 2, 128, 512), b16),
            jax.ShapeDtypeStruct((768, 128), b16),
            jax.ShapeDtypeStruct((8, 128), f32),
        ),
        in_specs=[pl.BlockSpec(memory_space=pl.ANY)] * 5
        + [pl.BlockSpec(memory_space=pltpu.VMEM)] * 5,
        out_specs=[pl.BlockSpec(memory_space=pltpu.VMEM)] * 3,
        scratch_shapes=[
            vmem((keep, 2 * rows.shape[1], 128), f32),
            vmem((768, 512), b16),
            vmem((2, 8, 2, 2, 128, 512), b16),
            vmem((2, 2, 2, 4, 128, 512), b16),
            vmem((2, number, 512), f32),
            vmem((2, number, 512), f32),
            vmem((2, 3, number, 512), b16),
            vmem((2, pairs, 2, 512), f32),
            vmem((2, number, 512), b16),
            vmem((2, 4, number, 512), b16),
            vmem((number, 512), f32),
            vmem((4, number, 512), b16),
            vmem((number, 512), b16),
            vmem((number, 512), b16),
            vmem((number, 512), b16),
            vmem((128, 512), f32),
            vmem((16, 512), f32),
            vmem((2, 2, 768, 128), b16),
            vmem((2 * levels + 1, 8, 128), f32),
        ]
        + [vmem(shape, b16) for shape in landing]
        + [
            dma((13, 5)),
            dma((13, 5)),
            dma((2, 9)),
            dma((2,)),
            dma((1,)),
            dma((13, steps)),
            dma((13, steps)),
            dma((levels,)),
            dma((levels,)),
            pltpu.SemaphoreType.REGULAR((2,)),
            pltpu.SemaphoreType.REGULAR((2,)),
            pltpu.SemaphoreType.REGULAR((2,)),
        ],
        compiler_params=pltpu.CompilerParams(
            collective_id=0, has_side_effects=True, vmem_limit_bytes=VMEM_LIMIT
        ),
    )(rows, *weights, *smalls)


def advance(weight, gradient, momentum, average, step_rate):
    new_momentum = MOMENTUM_KEEP * momentum + gradient
    new_weight = weight - step_rate * (gradient + MOMENTUM_KEEP * new_momentum)
    new_average = AVERAGE_KEEP * average + (1.0 - AVERAGE_KEEP) * new_weight
    return (new_weight, new_momentum, new_average)


def update_kernel(step_rate, wide_grad, tall_grad, small_grad, sums, *refs):
    inputs, outputs = refs[:27], refs[27:]
    scale = 1.0 / sums[0:1, 1:2]

    def put(member, place, gradient):
        entry = [inputs[9 * part + member][place] for part in range(3)]
        results = advance(entry[0], wide(gradient) * scale, entry[1], entry[2], step_rate)
        for part in range(3):
            outputs[9 * part + member][place] = results[part]

    places = (8, 9, 10, 11, 0, 1, 2, 3)
    for j in range(8):
        member = 0 if j < 3 else (1 if j == 3 else 2)
        column = 512 * (j if j < 3 else (0 if j == 3 else j - 4))
        gradient = wide_grad[0, places[j] if j < 4 else j - 4]
        put(member, (0, slice(None), slice(column, column + 512)), gradient)
    put(3, (0,), tall_grad[0, 0])

    @pl.when((pl.program_id(0) == 0) & (pl.program_id(1) == 0))
    def _():
        put(4, (...,), small_grad[640:648])
        put(5, (...,), small_grad[0:64])
        put(6, (...,), small_grad[64:128])
        put(7, (...,), small_grad[128:640])
        put(8, (...,), small_grad[648:650])


def update_call(big, small, sums, params, moments, averages, step_rate):
    big = big.reshape(2, 12, 128, 512)

    def block(rows, columns):
        return pl.BlockSpec((1, rows, columns), lambda l, i: (l, i, 0))

    def whole(*shape):
        return pl.BlockSpec(shape, lambda l, i: (0,) * len(shape))

    one_set = [
        block(32, 1536),
        block(32, 512),
        block(32, 2048),
        block(128, 512),
        whole(8, 128),
        whole(64, 128),
        whole(64, 128),
        whole(512, 128),
        whole(2, 128),
    ]
    arrays = []
    for group in (params, moments, averages):
        group = list(group)
        group[4] = group[4].reshape(8, 128)
        arrays += group
    out = pl.pallas_call(
        functools.partial(update_kernel, step_rate),
        grid=(2, 4),
        out_shape=[jax.ShapeDtypeStruct(array.shape, jnp.float32) for array in arrays],
        in_specs=[
            pl.BlockSpec((1, 12, 32, 512), lambda l, i: (1 - l, 0, i, 0)),
            pl.BlockSpec((1, 1, 128, 512), lambda l, i: (1 - l, 4 + i, 0, 0)),
            whole(768, 128),
            whole(8, 128),
        ]
        + one_set * 3,
        out_specs=one_set * 3,
        compiler_params=pltpu.CompilerParams(vmem_limit_bytes=VMEM_LIMIT),
    )(big, big, small, sums, *arrays)
    out = list(out)
    for part in range(3):
        out[9 * part + 4] = out[9 * part + 4].reshape(2, 4, 128)
    return out


def per_device(series_data, patch_mask, *state):
    params, moments, averages = state[:9], state[9:18], state[18:]
    total_series = series_data.shape[0] * lax.axis_size("dp") * lax.axis_size("fsdp")
    step_rate = RATE_FACTOR * math.sqrt(total_series * PATCHES)
    series_num, local_count = patch_mask.shape
    patches = series_data.reshape(series_num, local_count, PATCH)
    masked = jnp.broadcast_to(patch_mask.astype(jnp.float32)[..., None], patches.shape)
    rows = jnp.concatenate([patches, masked], axis=-1)
    qkv, out, up, down, norms, embed_w, head, pos, final = params
    big, small, sums = mega_call(
        rows,
        (qkv, out, up, down),
        (embed_w, head, pos, norms.reshape(8, 128), final),
        lax.axis_size("dp"),
    )
    new = update_call(big, small, sums, params, moments, averages, step_rate)
    return (sums[0, 0], sums[0, 1], *new)


def solution(mesh):
    matrix_spec = P(None, "fsdp", None)
    column = P(None, "fsdp")
    one_set = (matrix_spec,) * 4 + (P(None, None, "fsdp"),) + (column,) * 4
    data = P(("dp", "fsdp"), "seq")
    return jax.shard_map(
        per_device,
        mesh=mesh,
        in_specs=(data, data) + one_set * 3,
        out_specs=(P(), P()) + one_set * 3,
        check_vma=False,
    )
```

```python
import functools
import math

import jax
import jax.numpy as jnp
from jax import lax
from jax.experimental import pallas as pl
from jax.experimental.pallas import tpu as pltpu
from jax.sharding import PartitionSpec as P

D = 512
HEADS = 8
HEAD_DIM = 64
PATCH = 64
PATCHES = 512
LAYERS = 2
NORM_EPS = 1e-05
SCORE_SCALE = 0.125
MOMENTUM_KEEP = 0.9
AVERAGE_KEEP = 0.9
RATE_FACTOR = 0.5
MESH = pl.DeviceIdType.MESH
VMEM_LIMIT = 63 * 2**20


def flip(index, bit):
    return index + bit - 2 * bit * ((index // bit) % 2)


def position():
    return lax.axis_index("dp"), lax.axis_index("seq"), lax.axis_index("fsdp")


def bits_of(extent):
    found = []
    bit = 1
    while bit < extent:
        found.append(bit)
        bit *= 2
    return found


def greet(partners):
    barrier = pltpu.get_barrier_semaphore()
    for partner in partners:
        pl.semaphore_signal(barrier, inc=1, device_id=partner, device_id_type=MESH)
    pl.semaphore_wait(barrier, len(partners))


def remote(src, dst, send_sem, recv_sem, partner):
    return pltpu.make_async_remote_copy(
        src_ref=src,
        dst_ref=dst,
        send_sem=send_sem,
        recv_sem=recv_sem,
        device_id=partner,
        device_id_type=MESH,
    )

RB = 512
SERIES_ROWS = 512
GELU_A = math.sqrt(2.0 / math.pi)
GELU_B = 0.044715


def dot_nn(left, right):
    return jnp.dot(left, right, preferred_element_type=jnp.float32)


def dot_nt(left, right):
    return lax.dot_general(left, right, (((1,), (1,)), ((), ())), preferred_element_type=jnp.float32)


def dot_tn(left, right):
    return lax.dot_general(left, right, (((0,), (0,)), ((), ())), preferred_element_type=jnp.float32)


def low(value):
    return value.astype(jnp.bfloat16)


def wide(value):
    return value.astype(jnp.float32)


def normalise(rows):
    centred = rows - jnp.mean(rows, axis=-1, keepdims=True)
    variance = jnp.mean(centred * centred, axis=-1, keepdims=True)
    inverse = lax.rsqrt(variance + NORM_EPS)
    return centred * inverse, inverse


def norm_back(grad_rows, scaled, inverse, gain):
    inner = grad_rows * gain
    first = jnp.mean(inner, axis=-1, keepdims=True)
    second = jnp.mean(inner * scaled, axis=-1, keepdims=True)
    return inverse * (inner - first - scaled * second)


def column_sum(value):
    return jnp.sum(value, axis=0, keepdims=True)


def matrix(square, l, j):
    return square[l, j].reshape(512, 512)


def row_block(index, size=RB):
    return pl.ds(pl.multiple_of(index * size, size), size)


def forward_in(l, refs, hook):
    small, square, tall, hid, mid, qkv, lse, ctx, up = refs
    gain, bias = wide(small[640 + 4 * l : 641 + 4 * l]), wide(small[641 + 4 * l : 642 + 4 * l])

    def body(i, carry):
        r = row_block(i)
        normed = low(normalise(hid[l, r])[0] * gain + bias)
        for j in range(3):
            got = dot_nn(normed, matrix(square, l, j))
            if j == 0:
                got = got * SCORE_SCALE
            qkv[l, j, r] = low(got)
        return carry

    split_loop(body, hid.shape[1] // RB, 2, hook, 2.4)


def pair_slices(index):
    series, pair = index // 4, index % 4
    return row_block(series, SERIES_ROWS), pl.ds(pl.multiple_of(128 * pair, 128), 128)


def head_mask(block, head):
    lane = lax.broadcasted_iota(jnp.int32, block.shape, 1)
    keep = lane < HEAD_DIM if head == 0 else lane >= HEAD_DIM
    return jnp.where(keep, block, jnp.zeros_like(block))


def forward_attention(l, refs, hook):
    small, square, tall, hid, mid, qkv, lse, ctx, up = refs

    def body(step, carry):
        loaded = []
        for sub in range(2):
            r, columns = pair_slices(2 * step + sub)
            loaded.append([qkv[l, part, r, columns] for part in range(3)])
        order = [(sub, head) for sub in range(2) for head in range(2)]
        scores = {}

        def ask(at):
            if at < len(order):
                sub, head = order[at]
                query, key, value = loaded[sub]
                scores[at] = dot_nt(head_mask(key, head), query)

        for at in range(2):
            ask(at)
        parts = []
        for at, (sub, head) in enumerate(order):
            ask(at + 2)
            index = 2 * step + sub
            r, columns = pair_slices(index)
            found = scores.pop(at)
            value_t = loaded[sub][2].T
            top = jnp.max(found, axis=0, keepdims=True)
            weights = jnp.exp(found - top)
            total = column_sum(weights)
            lse[l, index, head : head + 1] = top + jnp.log(total)
            part = dot_nn(value_t[64 * head : 64 * head + 64], low(weights))
            parts.append(part * (1.0 / total))
            if head == 1:
                ctx[l, r, columns] = low(jnp.concatenate(parts, axis=0).T)
                parts = []
        return carry

    split_loop(body, lse.shape[1] // 2, 8 // 2, hook, 6.9)


def forward_out(l, refs, target, act, hook):
    small, square, tall, hid, mid, qkv, lse, ctx, up = refs
    gain, bias = wide(small[642 + 4 * l : 643 + 4 * l]), wide(small[643 + 4 * l : 644 + 4 * l])

    def body(i, carry):
        r = row_block(i, 512)
        middle = hid[l, r] + dot_nn(ctx[l, r], matrix(square, l, 3))
        mid[l, r] = middle
        normed = low(normalise(middle)[0] * gain + bias)
        result = middle
        raises = [dot_nn(normed, matrix(square, l, 4 + j)) for j in range(1)]
        for j in range(4):
            if j + 1 < 4:
                raises.append(dot_nn(normed, matrix(square, l, 4 + j + 1)))
            raised = raises[j]
            up[l, j, r] = low(raised)
            bend = jnp.tanh(raised * (GELU_A + (GELU_A * GELU_B) * raised * raised))
            halved = 0.5 * raised
            active = low(halved + halved * bend)
            if l == LAYERS - 1:
                act[j, r] = active
            result = result + dot_nn(active, tall[l, j // 2, j % 2].reshape(512, 512))
        target[r] = result
        return carry

    split_loop(body, hid.shape[1] // 512, 2, hook, 6.1)


def masked_input(block):
    lane = lax.broadcasted_iota(jnp.int32, block.shape, 1)
    hidden = block * (1.0 - pltpu.roll(block, 64, 1))
    return low(jnp.where(lane < PATCH, hidden, 0.0))


def split_loop(body, count, parts, hook, cost):
    size = count // parts
    for part in range(parts):
        lax.fori_loop(part * size, (part + 1) * size, body, 0)
        hook(cost / parts)


def embed(rows, small, hid):
    def body(i, carry):
        r = row_block(i)
        place = pl.ds(pl.multiple_of(128 + (i * RB) % PATCHES, 128), RB)
        hid[0, r] = dot_nn(masked_input(rows[r]), small[0:128]) + wide(small[place])
        return carry

    lax.fori_loop(0, hid.shape[1] // RB, body, 0)


def top(rows, small, grad, head_grad, norm_grad, sums):
    gain, bias = wide(small[648:649]), wide(small[649:650])
    head_grad[...] = jnp.zeros_like(head_grad)

    def body(i, carry):
        loss, count, gain_sum, bias_sum = carry
        r = row_block(i)
        block = rows[r]
        lane = lax.broadcasted_iota(jnp.int32, block.shape, 1)
        mask = jnp.where(lane >= PATCH, block, 0.0)
        scaled, inverse = normalise(grad[r])
        final = low(scaled * gain + bias)
        errors = dot_nt(final, small[0:128]) - pltpu.roll(block, 64, 1)
        wrong = errors * mask
        pull = low(2.0 * wrong)
        head_grad[...] += dot_tn(pull, final)
        below = dot_nn(pull, small[0:128])
        grad[r] = norm_back(below, scaled, inverse, gain)
        return (
            loss + column_sum(errors * wrong),
            count + column_sum(mask),
            gain_sum + column_sum(below * scaled),
            bias_sum + column_sum(below),
        )

    zero, line = jnp.zeros((1, 512), jnp.float32), jnp.zeros((1, 128), jnp.float32)
    loss, count, gain_sum, bias_sum = lax.fori_loop(
        0, grad.shape[0] // RB, body, (line, line, zero, zero)
    )
    norm_grad[8:9] = gain_sum
    norm_grad[9:10] = bias_sum
    lane = lax.broadcasted_iota(jnp.int32, (8, 128), 1)
    sums[...] = jnp.where(lane == 0, jnp.sum(loss), jnp.where(lane == 1, jnp.sum(count), 0.0))


def backward_mlp(l, refs, grad, act, back16, normed16, dctx, norm_grad, hook):
    small, square, tall, hid, mid, qkv, lse, ctx, up = refs
    gain, bias = wide(small[642 + 4 * l : 643 + 4 * l]), wide(small[643 + 4 * l : 644 + 4 * l])

    def body(i, carry):
        r = row_block(i)
        upstream = grad[r]
        upstream16 = low(upstream)
        if l < LAYERS - 1:
            back16[r] = upstream16
        below = jnp.zeros((RB, 512), jnp.float32)

        def pull(j):
            return dot_nt(upstream16, tall[l, j // 2, j % 2].reshape(512, 512))

        pulls = [pull(0), pull(1)]
        for j in range(4):
            if j < 2:
                pulls.append(pull(j + 2))
            pulled = wide(low(pulls[j]))
            raised = wide(up[l, j, r])
            square_u = raised * raised
            bend = jnp.tanh(raised * (GELU_A + (GELU_A * GELU_B) * square_u))
            half = 0.5 + 0.5 * bend
            if l < LAYERS - 1:
                act[j, r] = low(raised * half)
            slope = half + (raised * (0.5 * GELU_A + (1.5 * GELU_A * GELU_B) * square_u)) * (
                1.0 - bend * bend
            )
            inner = low(pulled * slope)
            up[l, j, r] = inner
            below = below + dot_nt(inner, matrix(square, l, 4 + j))
        scaled, inverse = normalise(mid[l, r])
        middle = upstream + norm_back(below, scaled, inverse, gain)
        grad[r] = middle
        normed16[r] = low(scaled * gain + bias)
        dctx[r] = low(dot_nt(low(middle), matrix(square, l, 3)))
        norm_grad[4 * l + 2 : 4 * l + 3] += column_sum(below * scaled)
        norm_grad[4 * l + 3 : 4 * l + 4] += column_sum(below)
        return carry

    split_loop(body, grad.shape[0] // RB, 2, hook, 7.5)


def weights_down(grad, act, places, allow, hook):
    back = low(grad[...])
    for j in range(4):
        tile = low(dot_tn(act[j], back)).reshape(2, 2, 128, 512)
        for half in range(2):
            places[half][j // 2, j % 2] = tile[half]
    allow()
    hook(2.3)


def weights_mlp(l, refs, grad, act, back16, normed16, ready, allow, hook):
    small, square, tall, hid, mid, qkv, lse, ctx, up = refs
    square[l, 3] = low(dot_tn(ctx[l], low(grad[...]))).reshape(2, 2, 128, 512)
    for j in range(4):
        tile = low(dot_tn(normed16[...], up[l, j]))
        square[l, 4 + j] = tile.reshape(2, 2, 128, 512)
    ready()
    if l == LAYERS - 1:
        allow(0, 1)
        hook(2.9)
        return
    allow(6, 7, (11, 1))
    hook(2.9)
    for j in range(4):
        tile = low(dot_tn(act[j], back16[...]))
        tall[l, j // 2, j % 2] = tile.reshape(4, 128, 512)
        if j == 1:
            hook(1.15)
    allow(8, 9)
    hook(1.15)


def backward_attention(l, refs, dctx, hook):
    small, square, tall, hid, mid, qkv, lse, ctx, up = refs

    def body(step, carry):
        loaded = []
        for sub in range(1):
            r, columns = pair_slices(1 * step + sub)
            loaded.append([qkv[l, part, r, columns] for part in range(3)] + [dctx[r, columns]])
        order = [(sub, head) for sub in range(1) for head in range(2)]
        products = {}

        def ask(at):
            if at < len(order):
                sub, head = order[at]
                query, key, value, pulled = loaded[sub]
                products[at] = (
                    dot_nt(head_mask(key, head), query),
                    dot_nt(head_mask(value, head), pulled),
                )

        for at in range(1):
            ask(at)
        queries_t, keys, values = [], [], []
        for at, (sub, head) in enumerate(order):
            ask(at + 1)
            index = 1 * step + sub
            query, key, value, pulled = loaded[sub]
            key_t = key.T
            scores, grad_weights = products.pop(at)
            weights = jnp.exp(scores - lse[l, index, head : head + 1])
            inner = weights * grad_weights
            grad_scores = low(inner - weights * column_sum(inner))
            values.append(dot_nn(low(weights), pulled))
            keys.append(dot_nn(grad_scores, query))
            queries_t.append(dot_nn(key_t[64 * head : 64 * head + 64], grad_scores))
            if head == 1:
                r, columns = pair_slices(index)
                lane = lax.broadcasted_iota(jnp.int32, (SERIES_ROWS, 128), 1)
                qkv[l, 0, r, columns] = low(jnp.concatenate(queries_t, axis=0).T * SCORE_SCALE)
                qkv[l, 1, r, columns] = low(jnp.where(lane < HEAD_DIM, keys[0], keys[1]))
                qkv[l, 2, r, columns] = low(jnp.where(lane < HEAD_DIM, values[0], values[1]))
                queries_t, keys, values = [], [], []
        return carry

    split_loop(body, lse.shape[1] // 1, 8, hook, 12.2)


def backward_in(l, refs, grad, normed16, norm_grad, hook):
    small, square, tall, hid, mid, qkv, lse, ctx, up = refs
    gain, bias = wide(small[640 + 4 * l : 641 + 4 * l]), wide(small[641 + 4 * l : 642 + 4 * l])

    def body(i, carry):
        r = row_block(i)
        below = dot_nt(qkv[l, 0, r], matrix(square, l, 0))
        for j in range(1, 3):
            below = below + dot_nt(qkv[l, j, r], matrix(square, l, j))
        scaled, inverse = normalise(hid[l, r])
        grad[r] = grad[r] + norm_back(below, scaled, inverse, gain)
        normed16[r] = low(scaled * gain + bias)
        norm_grad[4 * l : 4 * l + 1] += column_sum(below * scaled)
        norm_grad[4 * l + 1 : 4 * l + 2] += column_sum(below)
        return carry

    split_loop(body, grad.shape[0] // RB, 2, hook, 2.4)


def weights_in(l, j, refs, normed16):
    square, qkv = refs[1], refs[5]
    square[l, j] = low(dot_tn(normed16[...], qkv[l, j])).reshape(2, 2, 128, 512)


def small_grads(rows, grad, head_grad, norm_grad, store):
    def put(first, block):
        for owner in range(4):
            store[owner // 2, owner % 2, first : first + block.shape[0]] = low(
                block[:, 128 * owner : 128 * owner + 128]
            )

    total = head_grad[...]
    for i in range(rows.shape[0] // 512):
        r = slice(512 * i, 512 * i + 512)
        total = total + dot_tn(masked_input(rows[r]), low(grad[r]))
    put(0, total)
    summed = grad[0:512]
    for i in range(1, rows.shape[0] // 512):
        summed = summed + grad[512 * i : 512 * i + 512]
    put(128, summed)
    put(640, norm_grad[...])
    for owner in range(4):
        store[owner // 2, owner % 2, 656:768] = jnp.zeros((112, 128), jnp.bfloat16)


class Clock:
    RATES = {"core": 440e3, "y": 42e3, "x": 42e3, "z1": 42e3, "z2": 21e3}

    def __init__(self):
        self.now = 0.0
        self.free = dict.fromkeys(self.RATES, 0.0)

    def send(self, link, size):
        self.free[link] = max(self.free[link], self.now) + size / self.RATES[link]
        return self.free[link] + 3.0

    def reach(self, moment):
        self.now = max(self.now, moment)


def run_gather(clock, position_now, weights, smalls, square, tall, small, stage, sems):
    dp, seq, high, low_bit = position_now
    fsdp = 2 * high + low_bit
    send_sem, recv_sem, stage_sem = sems
    core = (dp, seq, 2 * high + 1 - low_bit)
    other = (dp, seq, 2 * (1 - high) + low_bit)
    twin = (dp, 1 - seq, fsdp)
    qkv_w, out_w, up_w, down_w = weights

    def lanes(owner):
        return pl.ds(pl.multiple_of(128 * owner, 128), 128)

    def small_full(y, c):
        return small.at[:, lanes(2 * y + c)]

    def small_part(y, c, half):
        return small.at[pl.ds(pl.multiple_of(384 * half, 128), 384), lanes(2 * y + c)]

    places = [(small_full, small_part)]
    for l in range(LAYERS):
        for first, number in ((0, 1), (1, 1), (2, 1), (3, 1), (4, 4)):
            places.append(
                (
                    lambda y, c, l=l, js=pl.ds(first, number): square.at[l, js, y, c],
                    lambda y, c, half, l=l, js=pl.ds(first, number): square.at[
                        l, js, y, c, pl.ds(pl.multiple_of(64 * half, 64), 64)
                    ],
                )
            )
        places.append(
            (
                lambda y, c, l=l: tall.at[l, y, c],
                lambda y, c, half, l=l: tall.at[l, y, c, pl.ds(2 * half, 2)],
            )
        )

    def copies(number):
        full, part = places[number]
        near, far = (high, low_bit), (1 - high, low_bit)
        moves = [
            (full(*near), core),
            (part(*near, seq), other),
            (part(*far, seq), twin),
            (part(*far, seq), core),
            (part(*far, 1 - seq), core),
        ]
        return [
            remote(ref, ref, send_sem.at[number, kind], recv_sem.at[number, kind], partner)
            for kind, (ref, partner) in enumerate(moves)
        ]

    every = [copies(number) for number in range(len(places))]

    staged = []
    for l in range(LAYERS):
        moves = [(qkv_w.at[l, :, pl.ds(512 * j, 512)], j, 1) for j in range(3)]
        moves += [(out_w.at[l], 3, 1)]
        moves += [(up_w.at[l, :, pl.ds(512 * j, 512)], 4 + j, 1) for j in range(4)]
        moves += [(down_w.at[l], 8, 4)]
        for index, (src, first, number) in enumerate(moves):
            dst = stage(l, first, number)
            copy = pltpu.make_async_copy(src, dst, stage_sem.at[l, index])
            copy.start()
            staged.append((copy, l, first, number, dst))

    embed_w, head_w, pos_w, norms_w, final_w = smalls
    mine = lanes(fsdp)
    small[0:64, mine] = low(embed_w[...])
    small[64:128, mine] = low(head_w[...])
    small[128:640, mine] = low(pos_w[...])
    small[640:656, mine] = low(jnp.concatenate([norms_w[...], final_w[...], jnp.zeros((6, 128))]))
    small[656:768, mine] = jnp.zeros((112, 128), jnp.bfloat16)

    def size(number):
        full = places[number][0](0, 0)
        return 2 * math.prod(full.shape)

    waiting = {}

    def launch(number):
        every[number][1].start()
        every[number][0].start()
        waiting[(1, number)] = clock.send("y", size(number) / 2)

    def launch_rest():
        ends = {0: 1, 1: 2, 2: 3, 3: 4, 7: 5, 8: 6}
        for copy, l, first, number, dst in staged:
            copy.wait()
            if first < 8:
                square[l, first, high, low_bit] = low(dst[...])
            else:
                tall[l, high, low_bit] = low(dst[...]).reshape(4, 128, 512)
            if first in ends:
                launch(6 * l + ends[first])

    def arrive(kind, number):
        clock.reach(waiting.pop((kind, number)))
        every[number][kind].wait_recv()
        if kind == 1:
            every[number][2].start()
            waiting[(2, number)] = clock.send("x", size(number) / 2)
            every[number][3].start()
        else:
            every[number][4].start()

    def soonest():
        return min(waiting, key=lambda entry: (waiting[entry], entry))

    def pump():
        while waiting and waiting[soonest()] <= clock.now:
            arrive(*soonest())

    def finish(number):
        while (1, number) in waiting or (2, number) in waiting:
            arrive(*soonest())
        for kind in (0, 3, 4):
            every[number][kind].wait_recv()

    def close():
        for entry in every:
            for copy in entry:
                copy.wait_send()

    return launch, launch_rest, pump, finish, close


EARLY_LINE = ()


def SMALL_LANDING(dp_bits):
    places, start, rows = [], 0, 768
    for step in range(3 + len(dp_bits)):
        if step == 0:
            size = 2 * 768
        else:
            if step > 1:
                rows = kept_rows(rows) or rows
            size = rows
        places.append((start, size))
        start += size
    return places


def kept_rows(rows):
    return rows // 2 if rows % 32 == 0 else 0


def run_reduce(clock, position_now, dp_bits, buffers, ready, sems):
    dp, seq, high, low_bit = position_now
    fsdp = 2 * high + low_bit
    partner_of = {
        "core": (dp, seq, 2 * high + 1 - low_bit),
        "y": (dp, seq, 2 * (1 - high) + low_bit),
        "x": (dp, 1 - seq, fsdp),
    }
    side_of = {"y": high, "x": seq}
    for bit in dp_bits:
        partner_of["z%d" % bit] = (flip(dp, bit), seq, fsdp)
        side_of["z%d" % bit] = (dp // bit) % 2
    square, tall, up, qkv, ctx, small_store, landing, spare, out_big, out_small = buffers
    ready_core, ready_other, ready_twin = ready
    send_sem, recv_sem = sems
    lines = ["z%d" % bit for bit in dp_bits]
    usual = ["y", "x"] + lines
    early = lines[:1] + ["y", "x"] + lines[1:]

    def describe_big(n, single=None):
        l, k = 1 - n // 6, n % 6
        down_first = l == 1 and k in (2, 3)
        if down_first:
            slots = [
                out_big.at[pl.ds(8 + 2 * (k - 2), 2)],
                out_big.at[6 + k - 2],
                out_big.at[5, k - 2],
            ]
            holds = [None, None, None]
        else:
            slots = [
                up.reshape(2, 8, 2, 2, 128, 512).at[l, k],
                ctx.reshape(2, 4, 2, 128, 512).at[1, n]
                if n < 2
                else qkv.reshape(2, 12, 2, 128, 512).at[1, n - 4],
                up.reshape(2, 32, 128, 512).at[l, 24 + k],
            ]
            holds = [ready_core.at[1 - l], ready_other.at[0 if n < 2 else 1], ready_twin.at[1 - l]]
        slots += [ref.at[n] for ref in landing[4:]]
        first = (4, 6, 0, 2, 0, 2)[k]
        if single is not None:
            slots = [slots[0].at[single], slots[1].at[single]] + [
                ref.at[pl.ds(ref.shape[0] // 2 * single, ref.shape[0] // 2)] for ref in slots[2:]
            ]
            return dict(
                source=lambda lane: square.at[l, first + single, :, lane],
                names="yr",
                rows=128,
                order=usual,
                slots=slots,
                holds=holds,
                final=out_big.at[n, single],
            )
        if down_first:
            source = lambda lane: spare[k - 2].at[:, lane]
        elif k in (2, 3):
            source = lambda lane: tall.at[l, :, lane, pl.ds(first, 2)]
        else:
            source = lambda lane: square.at[l, pl.ds(first, 2), :, lane]
        return dict(
            source=source,
            names="ytr" if k in (2, 3) else "tyr",
            rows=128,
            order=early if n in EARLY_LINE else usual,
            slots=slots,
            holds=holds,
            final=out_big.at[n],
        )

    chunks = {n: describe_big(n) for n in range(12)}
    for n in (10, 11):
        del chunks[n]
        for single in range(2):
            chunks[(n, single)] = describe_big(n, single)
    chunks["small"] = dict(
        source=lambda lane: small_store.at[:, lane],
        names="yr",
        rows=768,
        order=usual,
        slots=list(landing[:2]) + list(landing[2:4]) + list(landing[4:]),
        holds=[None] * 3,
        final=out_small,
    )
    small_slots = landing[0]
    numbers = {name: number for number, name in enumerate(chunks)}
    for name, chunk in chunks.items():
        chunk["steps"] = [("core", 0)]
        rows, names = chunk["rows"], chunk["names"]
        for link in chunk["order"]:
            if link == "y" or (link == "x" and "t" in names):
                names = names.replace("y" if link == "y" else "t", "")
                chunk["steps"].append((link, -1))
            else:
                kept = kept_rows(rows)
                rows = kept or rows
                chunk["steps"].append((link, kept))
        if name == "small":
            shapes = SMALL_LANDING(dp_bits)
            chunk["slots"] = [
                small_slots.at[pl.ds(start, size)] for start, size in shapes
            ]
    pending, started, due, waited = {}, [], {}, set()

    def begin(name, step, src, dst, link):
        n = numbers[name]
        copy = remote(src, dst, send_sem.at[n, step], recv_sem.at[n, step], partner_of[link])
        copy.start()
        started.append(copy)
        pending[name] = copy
        due[name] = clock.send(link if link in clock.RATES else "z2", 2 * math.prod(src.shape))

    def choose(ref, names, link, kept, side):
        if kept < 0:
            axis = names.index("y" if link == "y" else "t")
            return ref.at[(slice(None),) * axis + (side,)], names[:axis] + names[axis + 1 :]
        if kept == 0:
            return ref, names
        start = side * kept
        if not isinstance(start, int):
            start = pl.multiple_of(start, 16)
        return ref.at[(slice(None),) * names.index("r") + (pl.ds(start, kept),)], names

    state = {}

    def advance_chunk(name, step):
        chunk = chunks[name]
        steps = chunk["steps"]
        if step > 0:
            copy = pending.pop(name)
            copy.wait_recv()
            if name in (2, 3):
                copy.wait_send()
                started[:] = [entry for entry in started if entry is not copy]
        if step == 0:
            send, mine, names = chunk["source"](1 - low_bit), chunk["source"](low_bit), chunk["names"]
            state[name] = (mine, names)
        elif step <= len(steps):
            mine, names = state[name]
            link, kept = steps[step - 1]
            came = chunk["came"]
            came[...] += mine[...]
            if step == len(steps):
                place = chunk["final"]
                path, names = [], chunk["names"].replace("y", "")
                for link, kept in steps[1:]:
                    if link == "y":
                        continue
                    path.append((place, names, link, kept))
                    place, names = choose(place, names, link, kept, side_of[link])
                place[...] = came[...]
                chunk["back"] = [
                    (link, choose(place, names, link, kept, side_of[link])[0])
                    for place, names, link, kept in path[::-1]
                    if kept
                ]
            else:
                link, kept = steps[step]
                send = choose(came, names, link, kept, 1 - side_of[link])[0]
                state[name] = choose(came, names, link, kept, side_of[link])
        if step < len(steps):
            hold = chunk["holds"][step] if step < len(chunk["holds"]) else None
            if hold is not None:
                key = (step, chunk_hold_key(name, step))
                if key not in waited:
                    waited.add(key)
                    pl.semaphore_wait(hold, 1)
            slot = chunk["slots"][step]
            if len(slot.shape) == len(send.shape) == 2:
                slot = slot.at[pl.ds(0, send.shape[0])]
            chunk["came"] = slot.reshape(send.shape)
            begin(name, step, send, chunk["came"], steps[step][0])
            return
        turn = step - len(steps)
        if turn < len(chunk["back"]):
            link, piece = chunk["back"][turn]
            begin(name, step, piece, piece, link)

    def chunk_hold_key(name, step):
        n = name[0] if isinstance(name, tuple) else name
        if step == 1:
            return 0 if n < 2 else 1
        return n // 6

    progress = dict.fromkeys(chunks, 0)
    allowed = []

    def last(name):
        steps = chunks[name]["steps"]
        return len(steps) + sum(1 for link, kept in steps[1:] if link != "y" and kept)

    def move(name):
        clock.reach(due.pop(name, 0.0))
        advance_chunk(name, progress[name])
        clock.now += 0.2
        progress[name] += 1

    def open_chunks():
        return [name for name in allowed if progress[name] <= last(name)]

    def soonest():
        return min(open_chunks(), key=lambda name: (due.get(name, 0.0), allowed.index(name)))

    def tick():
        while open_chunks() and due.get(soonest(), 0.0) <= clock.now:
            move(soonest())

    def allow(*names):
        allowed.extend(names)

    def drain():
        while open_chunks():
            move(soonest())
        for copy in started:
            copy.wait_send()

    def ready_for(partner, semaphore):
        pl.semaphore_signal(semaphore, inc=1, device_id=partner_of[partner], device_id_type=MESH)

    def up_free(i):
        ready_for("core", ready_core.at[i])
        ready_for("x", ready_twin.at[i])

    return tick, allow, drain, up_free, lambda i: ready_for("y", ready_other.at[i])


def mega_kernel(dp_bits, landings, *refs):
    rows_in, qkv_w, out_w, up_w, down_w, embed_w, head_w, pos_w, norms_w, final_w = refs[:10]
    out_big, out_small, out_sums = refs[10:13]
    (rows, small, square, tall, hid, mid, qkv, lse, ctx, up, grad, act, back16, normed16, dctx,
     head_grad, norm_grad, small_store, loss_land) = refs[13:32]
    landing = refs[32 : 32 + landings]
    (gather_send, gather_recv, stage_sem, rows_sem, rows_local, reduce_send, reduce_recv, loss_send,
     loss_recv, ready_core, ready_other, ready_twin) = refs[32 + landings :]
    dp, seq, fsdp = position()
    high, low_bit = fsdp // 2, fsdp % 2
    place = (dp, seq, high, low_bit)
    core = (dp, seq, 2 * high + 1 - low_bit)
    other = (dp, seq, 2 * (1 - high) + low_bit)
    twin = (dp, 1 - seq, fsdp)
    partners = [core, other, twin] + [(flip(dp, bit), seq, fsdp) for bit in dp_bits]

    def stage(l, first, number):
        if first < 8:
            return mid.at[l, pl.ds(128 * first, 128 * number)]
        return (hid.at[1] if l == 0 else grad).at[pl.ds(0, 512)]

    clock = Clock()
    launch, launch_rest, pump, finish, close = run_gather(
        clock,
        place,
        (qkv_w, out_w, up_w, down_w),
        (embed_w, head_w, pos_w, norms_w, final_w),
        square,
        tall,
        small,
        stage,
        (gather_send, gather_recv, stage_sem),
    )
    greet(partners)
    launch(0)
    keep, local = rows_in.shape[0] // 2, rows_in.shape[1]
    mine = rows.at[:, pl.ds(pl.multiple_of(local * seq, local), local)]
    trade = remote(
        rows_in.at[pl.ds(keep * (1 - seq), keep)], mine, rows_sem.at[0], rows_sem.at[1], twin
    )
    trade.start()
    traded = clock.send("x", 4 * math.prod(rows_in.shape) // 2)
    own = pltpu.make_async_copy(rows_in.at[pl.ds(keep * seq, keep)], mine, rows_local.at[0])
    own.start()
    launch_rest()
    norm_grad[...] = jnp.zeros_like(norm_grad)
    finish(0)
    own.wait()
    trade.wait()
    clock.reach(traded)

    parts = (small, square, tall, hid, mid, qkv, lse, ctx, up)
    flat_rows = rows.reshape(rows.shape[0] * rows.shape[1], 128)
    def pump_after(cost):
        clock.now += cost
        pump()

    embed(flat_rows, small, hid)
    pump_after(1.2)
    for l in range(LAYERS):
        for number in range(6 * l + 1, 6 * l + 4):
            finish(number)
        forward_in(l, parts, pump_after)
        forward_attention(l, parts, pump_after)
        for number in range(6 * l + 4, 6 * l + 7):
            finish(number)
        forward_out(l, parts, hid.at[1] if l == 0 else grad, act, pump_after)
    close()
    top(flat_rows, small, grad, head_grad, norm_grad, loss_land.at[0])
    clock.now += 2.6

    spare = [
        back16.reshape(2, 2, 2, 128, 512),
        out_big.at[pl.ds(0, 4)].reshape(2, 2, 2, 128, 512),
    ]
    tick, allow, drain, ready_to_core, ready_to_other = run_reduce(
        clock,
        place,
        dp_bits,
        (square, tall, up, qkv, ctx, small_store, landing, spare, out_big, out_small),
        (ready_core, ready_other, ready_twin),
        (reduce_send, reduce_recv),
    )
    loss_state = {}
    loss_step = [0]

    def loss_tick():
        step = loss_step[0]
        if step > len(partners):
            return
        loss_step[0] += 1
        if step > 0:
            loss_state[step - 1].wait_recv()
            loss_land[2 * step] = loss_land[2 * step - 2] + loss_land[2 * step - 1]
        if step < len(partners):
            loss_state[step] = remote(
                loss_land.at[2 * step],
                loss_land.at[2 * step + 1],
                loss_send.at[step],
                loss_recv.at[step],
                partners[step],
            )
            loss_state[step].start()
        else:
            out_sums[...] = loss_land[2 * step]

    def hook(cost):
        clock.now += cost
        tick()
        loss_tick()

    for l in reversed(range(LAYERS)):
        before = 0 if l == 1 else 6
        if l == 1:
            weights_down(grad, act, spare, lambda: allow(2, 3), hook)
        backward_mlp(l, parts, grad, act, back16, normed16, dctx, norm_grad, hook)

        def ready():
            ready_to_core(1 - l)
            if l == 1:
                ready_to_other(0)

        weights_mlp(
            l, parts, grad, act, back16, normed16, ready, allow, hook
        )
        backward_attention(l, parts, dctx, hook)
        backward_in(l, parts, grad, normed16, norm_grad, hook)
        if l == 0:
            small_grads(flat_rows, grad, head_grad, norm_grad, small_store)
            allow("small")
            hook(0.7)
        for j in range(3):
            weights_in(l, j, parts, normed16)
            if l == 0:
                allow(((10, 0), (10, 1), (11, 0))[j])
                hook(0.67)
        if l == 1:
            ready_to_other(1)
            allow(4, 5)
            hook(2.0)
    while loss_step[0] <= len(partners):
        loss_tick()
    drain()
    for copy in loss_state.values():
        copy.wait_send()


def mega_call(rows, weights, smalls, dp_extent):
    dp_bits = bits_of(dp_extent)
    levels = 3 + len(dp_bits)
    number = rows.shape[0] * rows.shape[1]
    keep = rows.shape[0] // 2
    pairs = keep * 4
    f32, b16 = jnp.float32, jnp.bfloat16
    small_rows = sum(size for _, size in SMALL_LANDING(dp_bits))
    landing = [(small_rows, 128), (8, 128), (8, 128), (8, 128)]
    landing += [(12, max(32, 64 >> index), 512) for index in range(len(dp_bits))]
    vmem = pltpu.VMEM
    dma = pltpu.SemaphoreType.DMA
    steps = 5 + 2 * len(dp_bits)
    return pl.pallas_call(
        functools.partial(mega_kernel, dp_bits, len(landing)),
        out_shape=(
            jax.ShapeDtypeStruct((12, 2, 128, 512), b16),
            jax.ShapeDtypeStruct((768, 128), b16),
            jax.ShapeDtypeStruct((8, 128), f32),
        ),
        in_specs=[pl.BlockSpec(memory_space=pl.ANY)] * 5
        + [pl.BlockSpec(memory_space=pltpu.VMEM)] * 5,
        out_specs=[pl.BlockSpec(memory_space=pltpu.VMEM)] * 3,
        scratch_shapes=[
            vmem((keep, 2 * rows.shape[1], 128), f32),
            vmem((768, 512), b16),
            vmem((2, 8, 2, 2, 128, 512), b16),
            vmem((2, 2, 2, 4, 128, 512), b16),
            vmem((2, number, 512), f32),
            vmem((2, number, 512), f32),
            vmem((2, 3, number, 512), b16),
            vmem((2, pairs, 2, 512), f32),
            vmem((2, number, 512), b16),
            vmem((2, 4, number, 512), b16),
            vmem((number, 512), f32),
            vmem((4, number, 512), b16),
            vmem((number, 512), b16),
            vmem((number, 512), b16),
            vmem((number, 512), b16),
            vmem((128, 512), f32),
            vmem((16, 512), f32),
            vmem((2, 2, 768, 128), b16),
            vmem((2 * levels + 1, 8, 128), f32),
        ]
        + [vmem(shape, b16) for shape in landing]
        + [
            dma((13, 5)),
            dma((13, 5)),
            dma((2, 9)),
            dma((2,)),
            dma((1,)),
            dma((15, steps)),
            dma((15, steps)),
            dma((levels,)),
            dma((levels,)),
            pltpu.SemaphoreType.REGULAR((2,)),
            pltpu.SemaphoreType.REGULAR((2,)),
            pltpu.SemaphoreType.REGULAR((2,)),
        ],
        compiler_params=pltpu.CompilerParams(
            collective_id=0, has_side_effects=True, vmem_limit_bytes=VMEM_LIMIT
        ),
    )(rows, *weights, *smalls)


def advance(weight, gradient, momentum, average, step_rate):
    new_momentum = MOMENTUM_KEEP * momentum + gradient
    new_weight = weight - step_rate * (gradient + MOMENTUM_KEEP * new_momentum)
    new_average = AVERAGE_KEEP * average + (1.0 - AVERAGE_KEEP) * new_weight
    return (new_weight, new_momentum, new_average)


def update_kernel(step_rate, wide_grad, tall_grad, small_grad, sums, *refs):
    inputs, outputs = refs[:27], refs[27:]
    scale = 1.0 / sums[0:1, 1:2]

    def put(member, place, gradient):
        entry = [inputs[9 * part + member][place] for part in range(3)]
        results = advance(entry[0], wide(gradient) * scale, entry[1], entry[2], step_rate)
        for part in range(3):
            outputs[9 * part + member][place] = results[part]

    places = (8, 9, 10, 11, 0, 1, 2, 3)
    for j in range(8):
        member = 0 if j < 3 else (1 if j == 3 else 2)
        column = 512 * (j if j < 3 else (0 if j == 3 else j - 4))
        gradient = wide_grad[0, places[j] if j < 4 else j - 4]
        put(member, (0, slice(None), slice(column, column + 512)), gradient)
    put(3, (0,), tall_grad[0].reshape(256, 512))

    @pl.when((pl.program_id(0) == 0) & (pl.program_id(1) == 0))
    def _():
        put(4, (...,), small_grad[640:648])
        put(5, (...,), small_grad[0:64])
        put(6, (...,), small_grad[64:128])
        put(7, (...,), small_grad[128:640])
        put(8, (...,), small_grad[648:650])


def update_call(big, small, sums, params, moments, averages, step_rate):
    big = big.reshape(2, 12, 128, 512)

    def block(rows, columns):
        return pl.BlockSpec((1, rows, columns), lambda l, i: (l, i, 0))

    def whole(*shape):
        return pl.BlockSpec(shape, lambda l, i: (0,) * len(shape))

    one_set = [
        block(64, 1536),
        block(64, 512),
        block(64, 2048),
        block(256, 512),
        whole(8, 128),
        whole(64, 128),
        whole(64, 128),
        whole(512, 128),
        whole(2, 128),
    ]
    arrays = []
    for group in (params, moments, averages):
        group = list(group)
        group[4] = group[4].reshape(8, 128)
        arrays += group
    out = pl.pallas_call(
        functools.partial(update_kernel, step_rate),
        grid=(2, 2),
        out_shape=[jax.ShapeDtypeStruct(array.shape, jnp.float32) for array in arrays],
        in_specs=[
            pl.BlockSpec((1, 12, 64, 512), lambda l, i: (1 - l, 0, i, 0)),
            pl.BlockSpec((1, 2, 128, 512), lambda l, i: (1 - l, 2 + i, 0, 0)),
            whole(768, 128),
            whole(8, 128),
        ]
        + one_set * 3,
        out_specs=one_set * 3,
        compiler_params=pltpu.CompilerParams(vmem_limit_bytes=VMEM_LIMIT),
    )(big, big, small, sums, *arrays)
    out = list(out)
    for part in range(3):
        out[9 * part + 4] = out[9 * part + 4].reshape(2, 4, 128)
    return out


def per_device(series_data, patch_mask, *state):
    params, moments, averages = state[:9], state[9:18], state[18:]
    total_series = series_data.shape[0] * lax.axis_size("dp") * lax.axis_size("fsdp")
    step_rate = RATE_FACTOR * math.sqrt(total_series * PATCHES)
    series_num, local_count = patch_mask.shape
    patches = series_data.reshape(series_num, local_count, PATCH)
    masked = jnp.broadcast_to(patch_mask.astype(jnp.float32)[..., None], patches.shape)
    rows = jnp.concatenate([patches, masked], axis=-1)
    qkv, out, up, down, norms, embed_w, head, pos, final = params
    big, small, sums = mega_call(
        rows,
        (qkv, out, up, down),
        (embed_w, head, pos, norms.reshape(8, 128), final),
        lax.axis_size("dp"),
    )
    new = update_call(big, small, sums, params, moments, averages, step_rate)
    return (sums[0, 0], sums[0, 1], *new)


def solution(mesh):
    matrix_spec = P(None, "fsdp", None)
    column = P(None, "fsdp")
    one_set = (matrix_spec,) * 4 + (P(None, None, "fsdp"),) + (column,) * 4
    data = P(("dp", "fsdp"), "seq")
    return jax.shard_map(
        per_device,
        mesh=mesh,
        in_specs=(data, data) + one_set * 3,
        out_specs=(P(), P()) + one_set * 3,
        check_vma=False,
    )
```

```python
import functools
import math

import jax
import jax.numpy as jnp
from jax import lax
from jax.experimental import pallas as pl
from jax.experimental.pallas import tpu as pltpu
from jax.sharding import PartitionSpec as P

D = 512
HEADS = 8
HEAD_DIM = 64
PATCH = 64
PATCHES = 512
LAYERS = 2
NORM_EPS = 1e-05
SCORE_SCALE = 0.125
MOMENTUM_KEEP = 0.9
AVERAGE_KEEP = 0.9
RATE_FACTOR = 0.5
MESH = pl.DeviceIdType.MESH
VMEM_LIMIT = 63 * 2**20


def flip(index, bit):
    return index + bit - 2 * bit * ((index // bit) % 2)


def position():
    return lax.axis_index("dp"), lax.axis_index("seq"), lax.axis_index("fsdp")


def bits_of(extent):
    found = []
    bit = 1
    while bit < extent:
        found.append(bit)
        bit *= 2
    return found


def greet(partners):
    barrier = pltpu.get_barrier_semaphore()
    for partner in partners:
        pl.semaphore_signal(barrier, inc=1, device_id=partner, device_id_type=MESH)
    pl.semaphore_wait(barrier, len(partners))


def remote(src, dst, send_sem, recv_sem, partner):
    return pltpu.make_async_remote_copy(
        src_ref=src,
        dst_ref=dst,
        send_sem=send_sem,
        recv_sem=recv_sem,
        device_id=partner,
        device_id_type=MESH,
    )

RB = 512
SERIES_ROWS = 512
GELU_A = math.sqrt(2.0 / math.pi)
GELU_B = 0.044715


def dot_nn(left, right):
    return jnp.dot(left, right, preferred_element_type=jnp.float32)


def dot_nt(left, right):
    return lax.dot_general(left, right, (((1,), (1,)), ((), ())), preferred_element_type=jnp.float32)


def dot_tn(left, right):
    return lax.dot_general(left, right, (((0,), (0,)), ((), ())), preferred_element_type=jnp.float32)


def low(value):
    return value.astype(jnp.bfloat16)


def wide(value):
    return value.astype(jnp.float32)


def normalise(rows):
    centred = rows - jnp.mean(rows, axis=-1, keepdims=True)
    variance = jnp.mean(centred * centred, axis=-1, keepdims=True)
    inverse = lax.rsqrt(variance + NORM_EPS)
    return centred * inverse, inverse


def norm_back(grad_rows, scaled, inverse, gain):
    inner = grad_rows * gain
    first = jnp.mean(inner, axis=-1, keepdims=True)
    second = jnp.mean(inner * scaled, axis=-1, keepdims=True)
    return inverse * (inner - first - scaled * second)


def column_sum(value):
    return jnp.sum(value, axis=0, keepdims=True)


def matrix(square, l, j):
    return square[l, j].reshape(512, 512)


def row_block(index, size=RB):
    return pl.ds(pl.multiple_of(index * size, size), size)


def forward_in(l, refs, hook):
    small, square, tall, hid, mid, qkv, lse, ctx, up = refs
    gain, bias = wide(small[640 + 4 * l : 641 + 4 * l]), wide(small[641 + 4 * l : 642 + 4 * l])

    def body(i, carry):
        r = row_block(i)
        normed = low(normalise(hid[l, r])[0] * gain + bias)
        for j in range(3):
            got = dot_nn(normed, matrix(square, l, j))
            if j == 0:
                got = got * SCORE_SCALE
            qkv[l, j, r] = low(got)
        return carry

    split_loop(body, hid.shape[1] // RB, 2, hook, 2.4)


def pair_slices(index):
    series, pair = index // 4, index % 4
    return row_block(series, SERIES_ROWS), pl.ds(pl.multiple_of(128 * pair, 128), 128)


def head_mask(block, head):
    lane = lax.broadcasted_iota(jnp.int32, block.shape, 1)
    keep = lane < HEAD_DIM if head == 0 else lane >= HEAD_DIM
    return jnp.where(keep, block, jnp.zeros_like(block))


def forward_attention(l, refs, hook):
    small, square, tall, hid, mid, qkv, lse, ctx, up = refs

    def body(step, carry):
        loaded = []
        for sub in range(2):
            r, columns = pair_slices(2 * step + sub)
            loaded.append([qkv[l, part, r, columns] for part in range(3)])
        order = [(sub, head) for sub in range(2) for head in range(2)]
        scores = {}

        def ask(at):
            if at < len(order):
                sub, head = order[at]
                query, key, value = loaded[sub]
                scores[at] = dot_nt(head_mask(key, head), query)

        for at in range(2):
            ask(at)
        parts = []
        for at, (sub, head) in enumerate(order):
            ask(at + 2)
            index = 2 * step + sub
            r, columns = pair_slices(index)
            found = scores.pop(at)
            value_t = loaded[sub][2].T
            top = jnp.max(found, axis=0, keepdims=True)
            weights = jnp.exp(found - top)
            total = column_sum(weights)
            lse[l, index, head : head + 1] = top + jnp.log(total)
            part = dot_nn(value_t[64 * head : 64 * head + 64], low(weights))
            parts.append(part * (1.0 / total))
            if head == 1:
                ctx[l, r, columns] = low(jnp.concatenate(parts, axis=0).T)
                parts = []
        return carry

    split_loop(body, lse.shape[1] // 2, 8 // 2, hook, 6.9)


def forward_out(l, refs, target, act, hook):
    small, square, tall, hid, mid, qkv, lse, ctx, up = refs
    gain, bias = wide(small[642 + 4 * l : 643 + 4 * l]), wide(small[643 + 4 * l : 644 + 4 * l])

    def body(i, carry):
        r = row_block(i, 512)
        middle = hid[l, r] + dot_nn(ctx[l, r], matrix(square, l, 3))
        mid[l, r] = middle
        normed = low(normalise(middle)[0] * gain + bias)
        result = middle
        raises = [dot_nn(normed, matrix(square, l, 4 + j)) for j in range(1)]
        for j in range(4):
            if j + 1 < 4:
                raises.append(dot_nn(normed, matrix(square, l, 4 + j + 1)))
            raised = raises[j]
            up[l, j, r] = low(raised)
            bend = jnp.tanh(raised * (GELU_A + (GELU_A * GELU_B) * raised * raised))
            halved = 0.5 * raised
            active = low(halved + halved * bend)
            if l == LAYERS - 1:
                act[j, r] = active
            result = result + dot_nn(active, tall[l, j // 2, j % 2].reshape(512, 512))
        target[r] = result
        return carry

    split_loop(body, hid.shape[1] // 512, 2, hook, 6.1)


def masked_input(block):
    lane = lax.broadcasted_iota(jnp.int32, block.shape, 1)
    hidden = block * (1.0 - pltpu.roll(block, 64, 1))
    return low(jnp.where(lane < PATCH, hidden, 0.0))


def split_loop(body, count, parts, hook, cost):
    size = count // parts
    for part in range(parts):
        lax.fori_loop(part * size, (part + 1) * size, body, 0)
        hook(cost / parts)


def embed(rows, small, hid):
    def body(i, carry):
        r = row_block(i)
        place = pl.ds(pl.multiple_of(128 + (i * RB) % PATCHES, 128), RB)
        hid[0, r] = dot_nn(masked_input(rows[r]), small[0:128]) + wide(small[place])
        return carry

    lax.fori_loop(0, hid.shape[1] // RB, body, 0)


def top(rows, small, grad, head_grad, norm_grad, sums):
    gain, bias = wide(small[648:649]), wide(small[649:650])
    head_grad[...] = jnp.zeros_like(head_grad)

    def body(i, carry):
        loss, count, gain_sum, bias_sum = carry
        r = row_block(i)
        block = rows[r]
        lane = lax.broadcasted_iota(jnp.int32, block.shape, 1)
        mask = jnp.where(lane >= PATCH, block, 0.0)
        scaled, inverse = normalise(grad[r])
        final = low(scaled * gain + bias)
        errors = dot_nt(final, small[0:128]) - pltpu.roll(block, 64, 1)
        wrong = errors * mask
        pull = low(2.0 * wrong)
        head_grad[...] += dot_tn(pull, final)
        below = dot_nn(pull, small[0:128])
        grad[r] = norm_back(below, scaled, inverse, gain)
        return (
            loss + column_sum(errors * wrong),
            count + column_sum(mask),
            gain_sum + column_sum(below * scaled),
            bias_sum + column_sum(below),
        )

    zero, line = jnp.zeros((1, 512), jnp.float32), jnp.zeros((1, 128), jnp.float32)
    loss, count, gain_sum, bias_sum = lax.fori_loop(
        0, grad.shape[0] // RB, body, (line, line, zero, zero)
    )
    norm_grad[8:9] = gain_sum
    norm_grad[9:10] = bias_sum
    lane = lax.broadcasted_iota(jnp.int32, (8, 128), 1)
    sums[...] = jnp.where(lane == 0, jnp.sum(loss), jnp.where(lane == 1, jnp.sum(count), 0.0))


def backward_mlp(l, refs, grad, act, back16, normed16, dctx, norm_grad, hook):
    small, square, tall, hid, mid, qkv, lse, ctx, up = refs
    gain, bias = wide(small[642 + 4 * l : 643 + 4 * l]), wide(small[643 + 4 * l : 644 + 4 * l])

    def body(i, carry):
        r = row_block(i)
        upstream = grad[r]
        upstream16 = low(upstream)
        if l < LAYERS - 1:
            back16[r] = upstream16
        below = jnp.zeros((RB, 512), jnp.float32)

        def pull(j):
            return dot_nt(upstream16, tall[l, j // 2, j % 2].reshape(512, 512))

        pulls = [pull(0), pull(1)]
        for j in range(4):
            if j < 2:
                pulls.append(pull(j + 2))
            pulled = wide(low(pulls[j]))
            raised = wide(up[l, j, r])
            square_u = raised * raised
            bend = jnp.tanh(raised * (GELU_A + (GELU_A * GELU_B) * square_u))
            half = 0.5 + 0.5 * bend
            if l < LAYERS - 1:
                act[j, r] = low(raised * half)
            slope = half + (raised * (0.5 * GELU_A + (1.5 * GELU_A * GELU_B) * square_u)) * (
                1.0 - bend * bend
            )
            inner = low(pulled * slope)
            up[l, j, r] = inner
            below = below + dot_nt(inner, matrix(square, l, 4 + j))
        scaled, inverse = normalise(mid[l, r])
        middle = upstream + norm_back(below, scaled, inverse, gain)
        grad[r] = middle
        normed16[r] = low(scaled * gain + bias)
        dctx[r] = low(dot_nt(low(middle), matrix(square, l, 3)))
        norm_grad[4 * l + 2 : 4 * l + 3] += column_sum(below * scaled)
        norm_grad[4 * l + 3 : 4 * l + 4] += column_sum(below)
        return carry

    split_loop(body, grad.shape[0] // RB, 2, hook, 7.5)


def weights_down(grad, act, places, allow, hook):
    back = low(grad[...])
    for j in range(4):
        tile = low(dot_tn(act[j], back)).reshape(2, 2, 128, 512)
        for half in range(2):
            places[half][j // 2, j % 2] = tile[half]
    allow()
    hook(2.3)


def weights_mlp(l, refs, grad, act, back16, normed16, ready, allow, hook):
    small, square, tall, hid, mid, qkv, lse, ctx, up = refs
    square[l, 3] = low(dot_tn(ctx[l], low(grad[...]))).reshape(2, 2, 128, 512)
    for j in range(4):
        tile = low(dot_tn(normed16[...], up[l, j]))
        square[l, 4 + j] = tile.reshape(2, 2, 128, 512)
    ready()
    if l == LAYERS - 1:
        allow(0, 1)
        hook(2.9)
        return
    allow(6, 7, (11, 1))
    hook(2.9)
    for j in range(4):
        tile = low(dot_tn(act[j], back16[...]))
        tall[l, j // 2, j % 2] = tile.reshape(4, 128, 512)
        if j == 1:
            hook(1.15)
    allow(8, 9)
    hook(1.15)


def backward_attention(l, refs, dctx, hook):
    small, square, tall, hid, mid, qkv, lse, ctx, up = refs

    def body(step, carry):
        loaded = []
        for sub in range(1):
            r, columns = pair_slices(1 * step + sub)
            loaded.append([qkv[l, part, r, columns] for part in range(3)] + [dctx[r, columns]])
        order = [(sub, head) for sub in range(1) for head in range(2)]
        products = {}

        def ask(at):
            if at < len(order):
                sub, head = order[at]
                query, key, value, pulled = loaded[sub]
                products[at] = (
                    dot_nt(head_mask(key, head), query),
                    dot_nt(head_mask(value, head), pulled),
                )

        for at in range(1):
            ask(at)
        queries_t, keys, values = [], [], []
        for at, (sub, head) in enumerate(order):
            ask(at + 1)
            index = 1 * step + sub
            query, key, value, pulled = loaded[sub]
            key_t = key.T
            scores, grad_weights = products.pop(at)
            weights = jnp.exp(scores - lse[l, index, head : head + 1])
            inner = weights * grad_weights
            grad_scores = low(inner - weights * column_sum(inner))
            values.append(dot_nn(low(weights), pulled))
            keys.append(dot_nn(grad_scores, query))
            queries_t.append(dot_nn(key_t[64 * head : 64 * head + 64], grad_scores))
            if head == 1:
                r, columns = pair_slices(index)
                lane = lax.broadcasted_iota(jnp.int32, (SERIES_ROWS, 128), 1)
                qkv[l, 0, r, columns] = low(jnp.concatenate(queries_t, axis=0).T * SCORE_SCALE)
                qkv[l, 1, r, columns] = low(jnp.where(lane < HEAD_DIM, keys[0], keys[1]))
                qkv[l, 2, r, columns] = low(jnp.where(lane < HEAD_DIM, values[0], values[1]))
                queries_t, keys, values = [], [], []
        return carry

    split_loop(body, lse.shape[1] // 1, 8, hook, 12.2)


def backward_in(l, refs, grad, normed16, norm_grad, hook):
    small, square, tall, hid, mid, qkv, lse, ctx, up = refs
    gain, bias = wide(small[640 + 4 * l : 641 + 4 * l]), wide(small[641 + 4 * l : 642 + 4 * l])

    def body(i, carry):
        r = row_block(i)
        below = dot_nt(qkv[l, 0, r], matrix(square, l, 0))
        for j in range(1, 3):
            below = below + dot_nt(qkv[l, j, r], matrix(square, l, j))
        scaled, inverse = normalise(hid[l, r])
        grad[r] = grad[r] + norm_back(below, scaled, inverse, gain)
        normed16[r] = low(scaled * gain + bias)
        norm_grad[4 * l : 4 * l + 1] += column_sum(below * scaled)
        norm_grad[4 * l + 1 : 4 * l + 2] += column_sum(below)
        return carry

    split_loop(body, grad.shape[0] // RB, 2, hook, 2.4)


def weights_in(l, j, refs, normed16):
    square, qkv = refs[1], refs[5]
    square[l, j] = low(dot_tn(normed16[...], qkv[l, j])).reshape(2, 2, 128, 512)


def small_grads(rows, grad, head_grad, norm_grad, store):
    def put(first, block):
        for owner in range(4):
            store[owner // 2, owner % 2, first : first + block.shape[0]] = low(
                block[:, 128 * owner : 128 * owner + 128]
            )

    total = head_grad[...]
    for i in range(rows.shape[0] // 512):
        r = slice(512 * i, 512 * i + 512)
        total = total + dot_tn(masked_input(rows[r]), low(grad[r]))
    put(0, total)
    summed = grad[0:512]
    for i in range(1, rows.shape[0] // 512):
        summed = summed + grad[512 * i : 512 * i + 512]
    put(128, summed)
    put(640, norm_grad[...])
    for owner in range(4):
        store[owner // 2, owner % 2, 656:768] = jnp.zeros((112, 128), jnp.bfloat16)


class Clock:
    RATES = {"core": 440e3, "y": 42e3, "x": 42e3, "z1": 42e3, "z2": 21e3}

    def __init__(self):
        self.now = 0.0
        self.free = dict.fromkeys(self.RATES, 0.0)

    def send(self, link, size):
        self.free[link] = max(self.free[link], self.now) + size / self.RATES[link]
        return self.free[link] + 3.0

    def reach(self, moment):
        self.now = max(self.now, moment)


def run_gather(clock, position_now, weights, smalls, square, tall, small, stage, sems):
    dp, seq, high, low_bit = position_now
    fsdp = 2 * high + low_bit
    send_sem, recv_sem, stage_sem = sems
    core = (dp, seq, 2 * high + 1 - low_bit)
    other = (dp, seq, 2 * (1 - high) + low_bit)
    twin = (dp, 1 - seq, fsdp)
    qkv_w, out_w, up_w, down_w = weights

    def lanes(owner):
        return pl.ds(pl.multiple_of(128 * owner, 128), 128)

    def small_full(y, c):
        return small.at[:, lanes(2 * y + c)]

    def small_part(y, c, half):
        return small.at[pl.ds(pl.multiple_of(384 * half, 128), 384), lanes(2 * y + c)]

    places = [(small_full, small_part)]
    for l in range(LAYERS):
        for first, number in ((0, 1), (1, 1), (2, 1), (3, 1), (4, 4)):
            places.append(
                (
                    lambda y, c, l=l, js=pl.ds(first, number): square.at[l, js, y, c],
                    lambda y, c, half, l=l, js=pl.ds(first, number): square.at[
                        l, js, y, c, pl.ds(pl.multiple_of(64 * half, 64), 64)
                    ],
                )
            )
        places.append(
            (
                lambda y, c, l=l: tall.at[l, y, c],
                lambda y, c, half, l=l: tall.at[l, y, c, pl.ds(2 * half, 2)],
            )
        )

    def copies(number):
        full, part = places[number]
        near, far = (high, low_bit), (1 - high, low_bit)
        moves = [
            (full(*near), core),
            (part(*near, seq), other),
            (part(*far, seq), twin),
            (part(*far, seq), core),
            (part(*far, 1 - seq), core),
        ]
        return [
            remote(ref, ref, send_sem.at[number, kind], recv_sem.at[number, kind], partner)
            for kind, (ref, partner) in enumerate(moves)
        ]

    every = [copies(number) for number in range(len(places))]

    staged = []
    for l in range(LAYERS):
        moves = [(qkv_w.at[l, :, pl.ds(512 * j, 512)], j, 1) for j in range(3)]
        moves += [(out_w.at[l], 3, 1)]
        moves += [(up_w.at[l, :, pl.ds(512 * j, 512)], 4 + j, 1) for j in range(4)]
        moves += [(down_w.at[l], 8, 4)]
        for index, (src, first, number) in enumerate(moves):
            dst = stage(l, first, number)
            copy = pltpu.make_async_copy(src, dst, stage_sem.at[l, index])
            copy.start()
            staged.append((copy, l, first, number, dst))

    embed_w, head_w, pos_w, norms_w, final_w = smalls
    mine = lanes(fsdp)
    small[0:64, mine] = low(embed_w[...])
    small[64:128, mine] = low(head_w[...])
    small[128:640, mine] = low(pos_w[...])
    small[640:656, mine] = low(jnp.concatenate([norms_w[...], final_w[...], jnp.zeros((6, 128))]))
    small[656:768, mine] = jnp.zeros((112, 128), jnp.bfloat16)

    def size(number):
        full = places[number][0](0, 0)
        return 2 * math.prod(full.shape)

    waiting = {}

    def launch(number):
        every[number][1].start()
        every[number][0].start()
        waiting[(1, number)] = clock.send("y", size(number) / 2)

    def launch_rest():
        ends = {0: 1, 1: 2, 2: 3, 3: 4, 7: 5, 8: 6}
        for copy, l, first, number, dst in staged:
            copy.wait()
            if first < 8:
                square[l, first, high, low_bit] = low(dst[...])
            else:
                tall[l, high, low_bit] = low(dst[...]).reshape(4, 128, 512)
            if first in ends:
                launch(6 * l + ends[first])

    def arrive(kind, number):
        clock.reach(waiting.pop((kind, number)))
        every[number][kind].wait_recv()
        if kind == 1:
            every[number][2].start()
            waiting[(2, number)] = clock.send("x", size(number) / 2)
            every[number][3].start()
        else:
            every[number][4].start()

    def soonest():
        return min(waiting, key=lambda entry: (waiting[entry], entry))

    def pump():
        while waiting and waiting[soonest()] <= clock.now:
            arrive(*soonest())

    def finish(number):
        while (1, number) in waiting or (2, number) in waiting:
            arrive(*soonest())
        for kind in (0, 3, 4):
            every[number][kind].wait_recv()

    def close():
        for entry in every:
            for copy in entry:
                copy.wait_send()

    return launch, launch_rest, pump, finish, close


EARLY_LINE = ()


def SMALL_LANDING(dp_bits):
    places, start, rows = [], 0, 768
    for step in range(3 + len(dp_bits)):
        if step == 0:
            size = 2 * 768
        else:
            if step > 1:
                rows = kept_rows(rows) or rows
            size = rows
        places.append((start, size))
        start += size
    return places


def kept_rows(rows):
    return rows // 2 if rows % 32 == 0 else 0


def run_reduce(clock, position_now, dp_bits, buffers, ready, sems):
    dp, seq, high, low_bit = position_now
    fsdp = 2 * high + low_bit
    partner_of = {
        "core": (dp, seq, 2 * high + 1 - low_bit),
        "y": (dp, seq, 2 * (1 - high) + low_bit),
        "x": (dp, 1 - seq, fsdp),
    }
    side_of = {"y": high, "x": seq}
    for bit in dp_bits:
        partner_of["z%d" % bit] = (flip(dp, bit), seq, fsdp)
        side_of["z%d" % bit] = (dp // bit) % 2
    square, tall, up, qkv, ctx, small_store, landing, spare, out_big, out_small = buffers
    ready_core, ready_other, ready_twin = ready
    send_sem, recv_sem = sems
    lines = ["z%d" % bit for bit in dp_bits]
    usual = ["y", "x"] + lines
    early = lines[:1] + ["y", "x"] + lines[1:]

    def describe_big(n, single=None):
        l, k = 1 - n // 6, n % 6
        down_first = l == 1 and k in (2, 3)
        if down_first:
            slots = [
                out_big.at[pl.ds(8 + 2 * (k - 2), 2)],
                out_big.at[6 + k - 2],
                out_big.at[5, k - 2],
            ]
            holds = [None, None, None]
        else:
            slots = [
                up.reshape(2, 8, 2, 2, 128, 512).at[l, k],
                ctx.reshape(2, 4, 2, 128, 512).at[1, n]
                if n < 2
                else qkv.reshape(2, 12, 2, 128, 512).at[1, n - 4],
                up.reshape(2, 32, 128, 512).at[l, 24 + k],
            ]
            holds = [ready_core.at[1 - l], ready_other.at[0 if n < 2 else 1], ready_twin.at[1 - l]]
        slots += [ref.at[n] for ref in landing[4:]]
        first = (4, 6, 0, 2, 0, 2)[k]
        if single is not None:
            slots = [slots[0].at[single], slots[1].at[single]] + [
                ref.at[pl.ds(ref.shape[0] // 2 * single, ref.shape[0] // 2)] for ref in slots[2:]
            ]
            return dict(
                source=lambda lane: square.at[l, first + single, :, lane],
                names="yr",
                rows=128,
                order=usual,
                slots=slots,
                holds=holds,
                final=out_big.at[n, single],
            )
        if down_first:
            source = lambda lane: spare[k - 2].at[:, lane]
        elif k in (2, 3):
            source = lambda lane: tall.at[l, :, lane, pl.ds(first, 2)]
        else:
            source = lambda lane: square.at[l, pl.ds(first, 2), :, lane]
        return dict(
            source=source,
            names="ytr" if k in (2, 3) else "tyr",
            rows=128,
            order=early if n in EARLY_LINE else usual,
            slots=slots,
            holds=holds,
            final=out_big.at[n],
        )

    chunks = {n: describe_big(n) for n in range(12)}
    for n in (10, 11):
        del chunks[n]
        for single in range(2):
            chunks[(n, single)] = describe_big(n, single)
    chunks["small"] = dict(
        source=lambda lane: small_store.at[:, lane],
        names="yr",
        rows=768,
        order=usual,
        slots=list(landing[:2]) + list(landing[2:4]) + list(landing[4:]),
        holds=[None] * 3,
        final=out_small,
    )
    small_slots = landing[0]
    numbers = {name: number for number, name in enumerate(chunks)}
    for name, chunk in chunks.items():
        chunk["steps"] = [("core", 0)]
        rows, names = chunk["rows"], chunk["names"]
        for link in chunk["order"]:
            if link == "y" or (link == "x" and "t" in names):
                names = names.replace("y" if link == "y" else "t", "")
                chunk["steps"].append((link, -1))
            else:
                kept = kept_rows(rows)
                rows = kept or rows
                chunk["steps"].append((link, kept))
        if name == "small":
            shapes = SMALL_LANDING(dp_bits)
            chunk["slots"] = [
                small_slots.at[pl.ds(start, size)] for start, size in shapes
            ]
    pending, started, due, waited = {}, [], {}, set()

    def begin(name, step, src, dst, link):
        n = numbers[name]
        copy = remote(src, dst, send_sem.at[n, step], recv_sem.at[n, step], partner_of[link])
        copy.start()
        started.append(copy)
        pending[name] = copy
        due[name] = clock.send(link if link in clock.RATES else "z2", 2 * math.prod(src.shape))

    def choose(ref, names, link, kept, side):
        if kept < 0:
            axis = names.index("y" if link == "y" else "t")
            return ref.at[(slice(None),) * axis + (side,)], names[:axis] + names[axis + 1 :]
        if kept == 0:
            return ref, names
        start = side * kept
        if not isinstance(start, int):
            start = pl.multiple_of(start, 16)
        return ref.at[(slice(None),) * names.index("r") + (pl.ds(start, kept),)], names

    state = {}

    def advance_chunk(name, step):
        chunk = chunks[name]
        steps = chunk["steps"]
        if step > 0:
            copy = pending.pop(name)
            copy.wait_recv()
            if name in (2, 3):
                copy.wait_send()
                started[:] = [entry for entry in started if entry is not copy]
        if step == 0:
            send, mine, names = chunk["source"](1 - low_bit), chunk["source"](low_bit), chunk["names"]
            state[name] = (mine, names)
        elif step <= len(steps):
            mine, names = state[name]
            link, kept = steps[step - 1]
            came = chunk["came"]
            came[...] += mine[...]
            if step == len(steps):
                place = chunk["final"]
                path, names = [], chunk["names"].replace("y", "")
                for link, kept in steps[1:]:
                    if link == "y":
                        continue
                    path.append((place, names, link, kept))
                    place, names = choose(place, names, link, kept, side_of[link])
                place[...] = came[...]
                chunk["back"] = [
                    (link, choose(place, names, link, kept, side_of[link])[0])
                    for place, names, link, kept in path[::-1]
                    if kept
                ]
            else:
                link, kept = steps[step]
                send = choose(came, names, link, kept, 1 - side_of[link])[0]
                state[name] = choose(came, names, link, kept, side_of[link])
        if step < len(steps):
            hold = chunk["holds"][step] if step < len(chunk["holds"]) else None
            if hold is not None:
                key = (step, chunk_hold_key(name, step))
                if key not in waited:
                    waited.add(key)
                    pl.semaphore_wait(hold, 1)
            slot = chunk["slots"][step]
            if len(slot.shape) == len(send.shape) == 2:
                slot = slot.at[pl.ds(0, send.shape[0])]
            chunk["came"] = slot.reshape(send.shape)
            begin(name, step, send, chunk["came"], steps[step][0])
            return
        turn = step - len(steps)
        if turn < len(chunk["back"]):
            link, piece = chunk["back"][turn]
            begin(name, step, piece, piece, link)

    def chunk_hold_key(name, step):
        n = name[0] if isinstance(name, tuple) else name
        if step == 1:
            return 0 if n < 2 else 1
        return n // 6

    progress = dict.fromkeys(chunks, 0)
    allowed = []

    def last(name):
        steps = chunks[name]["steps"]
        return len(steps) + sum(1 for link, kept in steps[1:] if link != "y" and kept)

    def move(name):
        clock.reach(due.pop(name, 0.0))
        advance_chunk(name, progress[name])
        clock.now += 0.2
        progress[name] += 1

    def open_chunks():
        return [name for name in allowed if progress[name] <= last(name)]

    def soonest():
        return min(open_chunks(), key=lambda name: (due.get(name, 0.0), allowed.index(name)))

    def tick():
        while open_chunks() and due.get(soonest(), 0.0) <= clock.now:
            move(soonest())

    def allow(*names):
        allowed.extend(names)

    def drain():
        while open_chunks():
            move(soonest())
        for copy in started:
            copy.wait_send()

    def ready_for(partner, semaphore):
        pl.semaphore_signal(semaphore, inc=1, device_id=partner_of[partner], device_id_type=MESH)

    def up_free(i):
        ready_for("core", ready_core.at[i])
        ready_for("x", ready_twin.at[i])

    return tick, allow, drain, up_free, lambda i: ready_for("y", ready_other.at[i])


def mega_kernel(dp_bits, landings, *refs):
    rows_in, qkv_w, out_w, up_w, down_w, embed_w, head_w, pos_w, norms_w, final_w = refs[:10]
    out_big, out_small, out_sums = refs[10:13]
    (rows, small, square, tall, hid, mid, qkv, lse, ctx, up, grad, act, back16, normed16, dctx,
     head_grad, norm_grad, small_store, loss_land) = refs[13:32]
    landing = refs[32 : 32 + landings]
    (gather_send, gather_recv, stage_sem, rows_sem, rows_local, reduce_send, reduce_recv, loss_send,
     loss_recv, ready_core, ready_other, ready_twin) = refs[32 + landings :]
    dp, seq, fsdp = position()
    high, low_bit = fsdp // 2, fsdp % 2
    place = (dp, seq, high, low_bit)
    core = (dp, seq, 2 * high + 1 - low_bit)
    other = (dp, seq, 2 * (1 - high) + low_bit)
    twin = (dp, 1 - seq, fsdp)
    partners = [core, other, twin] + [(flip(dp, bit), seq, fsdp) for bit in dp_bits]

    def stage(l, first, number):
        if first < 8:
            return mid.at[l, pl.ds(128 * first, 128 * number)]
        return (hid.at[1] if l == 0 else grad).at[pl.ds(0, 512)]

    clock = Clock()
    launch, launch_rest, pump, finish, close = run_gather(
        clock,
        place,
        (qkv_w, out_w, up_w, down_w),
        (embed_w, head_w, pos_w, norms_w, final_w),
        square,
        tall,
        small,
        stage,
        (gather_send, gather_recv, stage_sem),
    )
    greet(partners)
    launch(0)
    keep, local = rows_in.shape[0] // 2, rows_in.shape[1]
    mine = rows.at[:, pl.ds(pl.multiple_of(local * seq, local), local)]
    trade = remote(
        rows_in.at[pl.ds(keep * (1 - seq), keep)], mine, rows_sem.at[0], rows_sem.at[1], twin
    )
    trade.start()
    traded = clock.send("x", 4 * math.prod(rows_in.shape) // 2)
    own = pltpu.make_async_copy(rows_in.at[pl.ds(keep * seq, keep)], mine, rows_local.at[0])
    own.start()
    launch_rest()
    norm_grad[...] = jnp.zeros_like(norm_grad)
    finish(0)
    own.wait()
    trade.wait()
    clock.reach(traded)

    parts = (small, square, tall, hid, mid, qkv, lse, ctx, up)
    flat_rows = rows.reshape(rows.shape[0] * rows.shape[1], 128)
    def pump_after(cost):
        clock.now += cost
        pump()

    embed(flat_rows, small, hid)
    pump_after(1.2)
    for l in range(LAYERS):
        for number in range(6 * l + 1, 6 * l + 4):
            finish(number)
        forward_in(l, parts, pump_after)
        forward_attention(l, parts, pump_after)
        for number in range(6 * l + 4, 6 * l + 7):
            finish(number)
        forward_out(l, parts, hid.at[1] if l == 0 else grad, act, pump_after)
    close()
    top(flat_rows, small, grad, head_grad, norm_grad, loss_land.at[0])
    clock.now += 2.6

    spare = [
        back16.reshape(2, 2, 2, 128, 512),
        out_big.at[pl.ds(0, 4)].reshape(2, 2, 2, 128, 512),
    ]
    tick, allow, drain, ready_to_core, ready_to_other = run_reduce(
        clock,
        place,
        dp_bits,
        (square, tall, up, qkv, ctx, small_store, landing, spare, out_big, out_small),
        (ready_core, ready_other, ready_twin),
        (reduce_send, reduce_recv),
    )
    loss_state = {}
    loss_step = [0]

    def loss_tick():
        step = loss_step[0]
        if step > len(partners):
            return
        loss_step[0] += 1
        if step > 0:
            loss_state[step - 1].wait_recv()
            loss_land[2 * step] = loss_land[2 * step - 2] + loss_land[2 * step - 1]
        if step < len(partners):
            loss_state[step] = remote(
                loss_land.at[2 * step],
                loss_land.at[2 * step + 1],
                loss_send.at[step],
                loss_recv.at[step],
                partners[step],
            )
            loss_state[step].start()
        else:
            out_sums[...] = loss_land[2 * step]

    def hook(cost):
        clock.now += cost
        tick()
        loss_tick()

    for l in reversed(range(LAYERS)):
        before = 0 if l == 1 else 6
        if l == 1:
            weights_down(grad, act, spare, lambda: allow(2, 3), hook)
        backward_mlp(l, parts, grad, act, back16, normed16, dctx, norm_grad, hook)

        def ready():
            ready_to_core(1 - l)
            if l == 1:
                ready_to_other(0)

        weights_mlp(
            l, parts, grad, act, back16, normed16, ready, allow, hook
        )
        backward_attention(l, parts, dctx, hook)
        backward_in(l, parts, grad, normed16, norm_grad, hook)
        if l == 0:
            small_grads(flat_rows, grad, head_grad, norm_grad, small_store)
            allow("small")
            hook(0.7)
        for j in range(3):
            weights_in(l, j, parts, normed16)
            if l == 0:
                allow(((10, 0), (10, 1), (11, 0))[j])
                hook(0.67)
        if l == 1:
            ready_to_other(1)
            allow(4, 5)
            hook(2.0)
    while loss_step[0] <= len(partners):
        loss_tick()
    drain()
    for copy in loss_state.values():
        copy.wait_send()


def mega_call(rows, weights, smalls, dp_extent):
    dp_bits = bits_of(dp_extent)
    levels = 3 + len(dp_bits)
    number = rows.shape[0] * rows.shape[1]
    keep = rows.shape[0] // 2
    pairs = keep * 4
    f32, b16 = jnp.float32, jnp.bfloat16
    small_rows = sum(size for _, size in SMALL_LANDING(dp_bits))
    landing = [(small_rows, 128), (8, 128), (8, 128), (8, 128)]
    landing += [(12, max(32, 64 >> index), 512) for index in range(len(dp_bits))]
    vmem = pltpu.VMEM
    dma = pltpu.SemaphoreType.DMA
    steps = 5 + 2 * len(dp_bits)
    return pl.pallas_call(
        functools.partial(mega_kernel, dp_bits, len(landing)),
        out_shape=(
            jax.ShapeDtypeStruct((12, 2, 128, 512), b16),
            jax.ShapeDtypeStruct((768, 128), b16),
            jax.ShapeDtypeStruct((8, 128), f32),
        ),
        in_specs=[pl.BlockSpec(memory_space=pl.ANY)] * 5
        + [pl.BlockSpec(memory_space=pltpu.VMEM)] * 5,
        out_specs=[pl.BlockSpec(memory_space=pltpu.VMEM)] * 3,
        scratch_shapes=[
            vmem((keep, 2 * rows.shape[1], 128), f32),
            vmem((768, 512), b16),
            vmem((2, 8, 2, 2, 128, 512), b16),
            vmem((2, 2, 2, 4, 128, 512), b16),
            vmem((2, number, 512), f32),
            vmem((2, number, 512), f32),
            vmem((2, 3, number, 512), b16),
            vmem((2, pairs, 2, 512), f32),
            vmem((2, number, 512), b16),
            vmem((2, 4, number, 512), b16),
            vmem((number, 512), f32),
            vmem((4, number, 512), b16),
            vmem((number, 512), b16),
            vmem((number, 512), b16),
            vmem((number, 512), b16),
            vmem((128, 512), f32),
            vmem((16, 512), f32),
            vmem((2, 2, 768, 128), b16),
            vmem((2 * levels + 1, 8, 128), f32),
        ]
        + [vmem(shape, b16) for shape in landing]
        + [
            dma((13, 5)),
            dma((13, 5)),
            dma((2, 9)),
            dma((2,)),
            dma((1,)),
            dma((15, steps)),
            dma((15, steps)),
            dma((levels,)),
            dma((levels,)),
            pltpu.SemaphoreType.REGULAR((2,)),
            pltpu.SemaphoreType.REGULAR((2,)),
            pltpu.SemaphoreType.REGULAR((2,)),
        ],
        compiler_params=pltpu.CompilerParams(
            collective_id=0, has_side_effects=True, vmem_limit_bytes=VMEM_LIMIT
        ),
    )(rows, *weights, *smalls)


def advance(weight, gradient, momentum, average, step_rate):
    new_momentum = MOMENTUM_KEEP * momentum + gradient
    new_weight = weight - step_rate * (gradient + MOMENTUM_KEEP * new_momentum)
    new_average = AVERAGE_KEEP * average + (1.0 - AVERAGE_KEEP) * new_weight
    return (new_weight, new_momentum, new_average)


def update_kernel(step_rate, wide_grad, tall_grad, small_grad, sums, *refs):
    inputs, outputs = refs[:27], refs[27:54]
    loss, count = refs[54:]
    scale = 1.0 / sums[0:1, 1:2]

    def put(member, place, gradient):
        entry = [inputs[9 * part + member][place] for part in range(3)]
        results = advance(entry[0], wide(gradient) * scale, entry[1], entry[2], step_rate)
        for part in range(3):
            outputs[9 * part + member][place] = results[part]

    places = (8, 9, 10, 11, 0, 1, 2, 3)
    for j in range(8):
        member = 0 if j < 3 else (1 if j == 3 else 2)
        column = 512 * (j if j < 3 else (0 if j == 3 else j - 4))
        gradient = wide_grad[0, places[j] if j < 4 else j - 4]
        put(member, (0, slice(None), slice(column, column + 512)), gradient)
    put(3, (0,), tall_grad[0].reshape(256, 512))

    @pl.when((pl.program_id(0) == 0) & (pl.program_id(1) == 0))
    def _():
        put(4, (...,), small_grad[640:648])
        put(5, (...,), small_grad[0:64])
        put(6, (...,), small_grad[64:128])
        put(7, (...,), small_grad[128:640])
        put(8, (...,), small_grad[648:650])
        loss[...] = sums[0:1, 0:1]
        count[...] = sums[0:1, 1:2]


def update_call(big, small, sums, params, moments, averages, step_rate):
    big = big.reshape(2, 12, 128, 512)

    def block(rows, columns):
        return pl.BlockSpec((1, rows, columns), lambda l, i: (l, i, 0))

    def whole(*shape):
        return pl.BlockSpec(shape, lambda l, i: (0,) * len(shape))

    one_set = [
        block(64, 1536),
        block(64, 512),
        block(64, 2048),
        block(256, 512),
        whole(8, 128),
        whole(64, 128),
        whole(64, 128),
        whole(512, 128),
        whole(2, 128),
    ]
    arrays = []
    for group in (params, moments, averages):
        group = list(group)
        group[4] = group[4].reshape(8, 128)
        arrays += group
    out = pl.pallas_call(
        functools.partial(update_kernel, step_rate),
        grid=(2, 2),
        out_shape=[jax.ShapeDtypeStruct(array.shape, jnp.float32) for array in arrays]
        + [jax.ShapeDtypeStruct((1, 1), jnp.float32)] * 2,
        in_specs=[
            pl.BlockSpec((1, 12, 64, 512), lambda l, i: (1 - l, 0, i, 0)),
            pl.BlockSpec((1, 2, 128, 512), lambda l, i: (1 - l, 2 + i, 0, 0)),
            whole(768, 128),
            whole(8, 128),
        ]
        + one_set * 3,
        out_specs=one_set * 3 + [whole(1, 1)] * 2,
        compiler_params=pltpu.CompilerParams(vmem_limit_bytes=VMEM_LIMIT),
    )(big, big, small, sums, *arrays)
    out = list(out)
    loss, count = out[27:]
    out = out[:27]
    for part in range(3):
        out[9 * part + 4] = out[9 * part + 4].reshape(2, 4, 128)
    return loss.reshape(()), count.reshape(()), *out


def per_device(series_data, patch_mask, *state):
    params, moments, averages = state[:9], state[9:18], state[18:]
    total_series = series_data.shape[0] * lax.axis_size("dp") * lax.axis_size("fsdp")
    step_rate = RATE_FACTOR * math.sqrt(total_series * PATCHES)
    series_num, local_count = patch_mask.shape
    patches = series_data.reshape(series_num, local_count, PATCH)
    masked = jnp.broadcast_to(patch_mask.astype(jnp.float32)[..., None], patches.shape)
    rows = jnp.concatenate([patches, masked], axis=-1)
    qkv, out, up, down, norms, embed_w, head, pos, final = params
    big, small, sums = mega_call(
        rows,
        (qkv, out, up, down),
        (embed_w, head, pos, norms.reshape(8, 128), final),
        lax.axis_size("dp"),
    )
    return update_call(big, small, sums, params, moments, averages, step_rate)


def solution(mesh):
    matrix_spec = P(None, "fsdp", None)
    column = P(None, "fsdp")
    one_set = (matrix_spec,) * 4 + (P(None, None, "fsdp"),) + (column,) * 4
    data = P(("dp", "fsdp"), "seq")
    return jax.shard_map(
        per_device,
        mesh=mesh,
        in_specs=(data, data) + one_set * 3,
        out_specs=(P(), P()) + one_set * 3,
        check_vma=False,
    )
```
